128 devices in a mesh: dp: 4 (over x), ctx: 16 (over z, y), head: 2 (over core).
Axes of the slice: x: 4, y: 4, z: 4, core: 2. Of those that a mesh axis runs over, the one named last changes fastest.
Arguments:
- queries: bfloat16 [16384, 32, 128], P(('dp', 'ctx'), 'head'), parts along dimension 0, may hold values from -112 to 112, as said below
- keys: bfloat16 [16384, 16, 128], P(('dp', 'ctx'), 'head'), parts along dimension 0, may hold values from -4 to 4, as said below
- values: bfloat16 [16384, 16, 128], P(('dp', 'ctx'), 'head'), parts along dimension 0, may hold values from -4 to 4
- out_grad: bfloat16 [16384, 32, 128], P(('dp', 'ctx'), 'head'), parts along dimension 0, may hold values from -4 to 4
- doc_lengths: int32 [128], P('dp'), parts along dimension 0, may hold values from 1 to 1024, 4096 in all
Outputs:
- attended: bfloat16 [16384, 32, 128], P(('dp', 'ctx'), 'head'), parts along dimension 0
- query_grad: bfloat16 [16384, 32, 128], P(('dp', 'ctx'), 'head'), parts along dimension 0
- key_grad: bfloat16 [16384, 16, 128], P(('dp', 'ctx'), 'head'), parts along dimension 0
- value_grad: bfloat16 [16384, 16, 128], P(('dp', 'ctx'), 'head'), parts along dimension 0
The draws below stay inside these ranges and needn't reach their ends.
There are 4 independent parts, one for each index of `dp`. The reference program is written for one: setup_inputs(seed, part) draws one part's arguments, and reference() takes and returns one part's arrays. A program takes and returns all parts, laid end to end along the dimension named above; each array names one. Nothing has to cross between parts.
Inputs may be any that keep to these rules, and one draw needn't show every extreme that they name: Entries of the queries lie in this range. Entries of the keys lie in this range. `doc_lengths`: the lengths sum to 4096; the longest document has exactly 1024 tokens.
All inputs are finite; a program needn't handle non-finite values.
Results may differ from the reference program's by a relative error of at most 0.0055.
Values may be sent and summed in bfloat16 or wider, within the bound.
No kernel may reach another device: no remote copies, remote signals or barrier semaphores. Data moves between devices by JAX's collectives and lax.ppermute only.
A program may use at most 192 MiB of HBM per device.

```python
import math
import jax
import jax.numpy as jnp
import numpy as np
from jax import lax

HEADS = 32
KV_HEADS = 16
HEAD_DIM = 128
WINDOW = 1024
TOK_DEV = 256
GROUP = 2
REACH = 4
ROW = 4096
DOCS = 32


def shared_keys(key):
    base_keys = jnp.clip(jax.random.normal(jax.random.fold_in(key, 21), (ROW, KV_HEADS, HEAD_DIM), jnp.float32), -4.0, 4.0)
    return base_keys


def draw_keys(key, part):
    base_keys = shared_keys(key)
    return base_keys.astype(jnp.bfloat16)


def draw_queries(key, part):
    drawn = jnp.clip(jax.random.normal(jax.random.fold_in(key, 31), (ROW, HEADS, HEAD_DIM), jnp.float32), -4.0, 4.0)
    return drawn.astype(jnp.bfloat16)


def levels(stream_key, dims, pieces, smallest, high):
    def one(position, shards_of):
        draws = jax.random.uniform(jax.random.fold_in(jax.random.fold_in(stream_key, 6), position), (shards_of,), jnp.float32, smallest / len(pieces), high / len(pieces))
        return jnp.repeat(jnp.exp(draws), dims[position] // shards_of).reshape((-1,) + (1,) * (len(dims) - position - 1))

    level = one(*pieces[0])
    for cut in pieces[1:]:
        level = level * one(*cut)
    return level


def profile(number_of, total, most, skew):
    portions = [(1 << 20) // math.isqrt(grade ** skew) + 1 for grade in range(2, number_of + 1)]
    spare, counts = total - most - (number_of - 1), [1] * (number_of - 1)
    while spare > 0:
        candidates = [i for i in range(number_of - 1) if counts[i] < most]
        whole, left = sum([portions[i] for i in candidates]), spare
        for i in candidates:
            extra = min(most - counts[i], max(1, left * portions[i] // whole), spare)
            counts[i] = counts[i] + extra
            spare = spare - extra
    return np.array([most] + counts)


def ragged(key, number_of, total, most, lean):
    if number_of == 2:
        one = jax.random.randint(key, (), max(1, total - most), min(most, total - 1) + 1)
        return jnp.stack([one, total - one])
    tallies = jnp.asarray(profile(number_of, total, most, lean), jnp.int32)
    couples = (number_of - 1) // 2
    source_of, sink = tallies[1:1 + 2 * couples:2], tallies[2:2 + 2 * couples:2]
    margin = jnp.minimum(source_of - 1, most - sink)
    moved = jax.random.randint(jax.random.fold_in(key, 1), (couples,), 0, 1 << 20) % (margin + 1)
    tallies = tallies.at[1:1 + 2 * couples:2].set(source_of - moved).at[2:2 + 2 * couples:2].set(sink + moved)
    return tallies[jax.random.permutation(jax.random.fold_in(key, 2), number_of)]


def normal_values(key, dims, deviation, reach, pieces=(), kind=jnp.bfloat16):
    level = levels(key, dims, pieces, -0.22, 0.18) if pieces else 1.0
    entries = jax.random.normal(key, dims, jnp.float32) * deviation * level
    return jnp.minimum(jnp.maximum(entries, -reach), reach).astype(kind)


def setup_inputs(seed: int = 0, part: int = 0) -> dict:
    seeds = jax.random.split(jax.random.key(seed), 6)
    own_keys = jax.random.split(jax.random.fold_in(seeds[5], part), 6)
    queries = draw_queries(jax.random.fold_in(jax.random.fold_in(seeds[5], part), 71), part)
    keys = draw_keys(jax.random.fold_in(jax.random.fold_in(seeds[5], part), 71), part)
    values = normal_values(own_keys[2], (ROW, KV_HEADS, HEAD_DIM), 1.0, 4.0, ((0, 16), (1, 2)))
    out_grad = normal_values(own_keys[3], (ROW, HEADS, HEAD_DIM), 1.0, 4.0, ((0, 16), (1, 2)))
    doc_lengths = ragged(own_keys[4], DOCS, ROW, ROW // 4, 2).astype(jnp.int32)
    return dict(queries=queries, keys=keys, values=values, out_grad=out_grad, doc_lengths=doc_lengths)


SCALING = 168.0 ** -0.5


def doc_index(positions, doc_lengths):
    ends = jnp.cumsum(doc_lengths).astype(jnp.int32)
    return jnp.sum((positions[:, None] >= ends[None, :]).astype(jnp.int32), axis=1)


def reference(queries, keys, values, out_grad, doc_lengths):
    row_length = queries.shape[0]
    halo_rows = REACH * TOK_DEV
    key_span = halo_rows + TOK_DEV
    padding = jnp.zeros((halo_rows, KV_HEADS, HEAD_DIM), keys.dtype)
    keys_padded = jnp.concatenate([padding, keys], 0)
    values_padded = jnp.concatenate([padding, values], 0)
    blocks = row_length // TOK_DEV

    def advance(running, block_index):
        key_acc, value_acc = running
        offset = (block_index * TOK_DEV).astype(jnp.int32)
        query_block = lax.dynamic_slice_in_dim(queries, offset, TOK_DEV, 0).astype(jnp.float32).reshape(TOK_DEV, KV_HEADS, GROUP, HEAD_DIM)
        grad_block = lax.dynamic_slice_in_dim(out_grad, offset, TOK_DEV, 0).astype(jnp.float32).reshape(TOK_DEV, KV_HEADS, GROUP, HEAD_DIM)
        key_block = lax.dynamic_slice_in_dim(keys_padded, offset, key_span, 0).astype(jnp.float32)
        value_block = lax.dynamic_slice_in_dim(values_padded, offset, key_span, 0).astype(jnp.float32)
        query_pos = offset + jnp.arange(TOK_DEV, dtype=jnp.int32)
        key_pos = offset - halo_rows + jnp.arange(key_span, dtype=jnp.int32)
        gap = query_pos[:, None] - key_pos[None, :]
        allowed = (gap >= 0) & (gap < WINDOW) & (key_pos[None, :] >= 0)
        allowed = allowed & (doc_index(query_pos, doc_lengths)[:, None] == doc_index(key_pos, doc_lengths)[None, :])
        scores = SCALING * jnp.einsum("qgjd,kgd->gjqk", query_block, key_block)
        maximum = jnp.max(jnp.where(allowed, scores, -jnp.inf), axis=3, keepdims=True)
        weights = jnp.where(allowed, jnp.exp(scores - maximum), 0.0)
        weights = weights / jnp.sum(weights, axis=3, keepdims=True)
        rounded = lax.optimization_barrier(weights.astype(jnp.bfloat16)).astype(jnp.float32)
        attended = jnp.einsum("gjqk,kgd->qgjd", rounded, value_block).astype(jnp.bfloat16)
        weight_grad = jnp.einsum("qgjd,kgd->gjqk", grad_block, value_block)
        row_total = jnp.sum(weights * weight_grad, axis=3, keepdims=True)
        score_grad = lax.optimization_barrier((weights * (weight_grad - row_total)).astype(jnp.bfloat16)).astype(jnp.float32)
        query_grad = (SCALING * jnp.einsum("gjqk,kgd->qgjd", score_grad, key_block)).astype(jnp.bfloat16)
        key_part = SCALING * jnp.einsum("gjqk,qgjd->kgd", score_grad, query_block)
        value_part = jnp.einsum("gjqk,qgjd->kgd", rounded, grad_block)
        key_acc = lax.dynamic_update_slice_in_dim(key_acc, lax.dynamic_slice_in_dim(key_acc, offset, key_span, 0) + key_part, offset, 0)
        value_acc = lax.dynamic_update_slice_in_dim(value_acc, lax.dynamic_slice_in_dim(value_acc, offset, key_span, 0) + value_part, offset, 0)
        return (key_acc, value_acc), (attended.reshape(TOK_DEV, HEADS, HEAD_DIM), query_grad.reshape(TOK_DEV, HEADS, HEAD_DIM))

    start_acc = jnp.zeros((halo_rows + row_length, KV_HEADS, HEAD_DIM), jnp.float32)
    (key_acc, value_acc), (attended, query_grad) = lax.scan(advance, (start_acc, start_acc), jnp.arange(blocks, dtype=jnp.int32))
    attended = attended.reshape(row_length, HEADS, HEAD_DIM)
    query_grad = query_grad.reshape(row_length, HEADS, HEAD_DIM)
    key_grad = key_acc[halo_rows:].astype(jnp.bfloat16)
    value_grad = value_acc[halo_rows:].astype(jnp.bfloat16)
    return (attended, query_grad, key_grad, value_grad)
```

```python
import functools

import jax
import jax.numpy as jnp
from jax import lax
from jax.experimental import pallas as pl
from jax.experimental.pallas import tpu as pltpu
from jax.sharding import PartitionSpec as P

WINDOW = 1024
SCALING = 168.0 ** (-0.5)
LOG2E = 1.4426950408889634
NEG = -1e30

NT = (((1,), (1,)), ((), ()))
NN = (((1,), (0,)), ((), ()))


def dot(a, b, dims):
    return lax.dot_general(a, b, dims, preferred_element_type=jnp.float32)


def attention_kernel(first_ref, ends_ref, x_ref, y_ref, kt_ref, vt_ref, dk_ref, dv_ref, s_ref, g_ref, *, blocks, rows):
    dk_ref[...] = jnp.zeros_like(dk_ref)
    dv_ref[...] = jnp.zeros_like(dv_ref)
    diff = lax.broadcasted_iota(jnp.int32, (rows, rows), 1) - lax.broadcasted_iota(jnp.int32, (rows, rows), 0)

    def transpose_step(t, carry):
        kt_ref[t] = x_ref[t, 2].T
        vt_ref[t] = x_ref[t, 3].T
        return carry

    lax.fori_loop(0, blocks, transpose_step, 0)

    def query_step(i, carry):
        q = x_ref[i, 0]
        do = x_ref[i, 1]
        first = first_ref[i]
        count = i - first + 1
        pos = i * rows + lax.broadcasted_iota(jnp.int32, (1, rows), 1)
        ends = ends_ref[...]
        start = jnp.max(jnp.where(ends <= pos, ends, 0), axis=0, keepdims=True)
        reach = pos - jnp.maximum(start, pos - (WINDOW - 1))

        def score_step(t, top):
            raw = dot(x_ref[first + t, 2], q, NT)
            gap = diff + (i - first - t) * rows
            raw = jnp.where((gap >= 0) & (gap <= reach), raw, NEG)
            s_ref[t] = raw
            return jnp.maximum(top, jnp.max(raw, axis=0, keepdims=True))

        top = lax.fori_loop(0, count, score_step, jnp.full((1, rows), NEG, jnp.float32))

        def weight_step(t, sums):
            total, mixed = sums
            p = jnp.exp2((s_ref[t] - top) * (SCALING * LOG2E))
            g = dot(x_ref[first + t, 3], do, NT)
            s_ref[t] = p
            g_ref[t] = g
            return (
                total + jnp.sum(p, axis=0, keepdims=True),
                mixed + jnp.sum(p * g, axis=0, keepdims=True),
            )

        zero = jnp.zeros((1, rows), jnp.float32)
        total, mixed = lax.fori_loop(0, count, weight_step, (zero, zero))
        inverse = 1.0 / total
        row_total = mixed * inverse

        def grad_step(t, sums):
            out, dq = sums
            w = s_ref[t] * inverse
            wb = w.astype(jnp.bfloat16)
            ds = (w * (g_ref[t] - row_total)).astype(jnp.bfloat16)
            out = out + dot(vt_ref[first + t], wb, NN)
            dq = dq + dot(kt_ref[first + t], ds, NN)
            dv_ref[first + t] += dot(wb, do, NN)
            dk_ref[first + t] += dot(ds, q, NN)
            return out, dq

        zeros = jnp.zeros((q.shape[1], rows), jnp.float32)
        out, dq = lax.fori_loop(0, count, grad_step, (zeros, zeros))
        y_ref[i, 0] = out.T.astype(jnp.bfloat16)
        y_ref[i, 1] = (SCALING * dq).T.astype(jnp.bfloat16)
        return carry

    lax.fori_loop(0, blocks, query_step, 0)

    def write_step(t, carry):
        y_ref[t, 2] = (SCALING * dk_ref[t]).astype(jnp.bfloat16)
        y_ref[t, 3] = dv_ref[t].astype(jnp.bfloat16)
        return carry

    lax.fori_loop(0, blocks, write_step, 0)


def attention(first, ends, x):
    blocks, _, rows, dim = x.shape
    tiles = WINDOW // rows + 1
    return pl.pallas_call(
        functools.partial(attention_kernel, blocks=blocks, rows=rows),
        out_shape=jax.ShapeDtypeStruct(x.shape, jnp.bfloat16),
        in_specs=[
            pl.BlockSpec(memory_space=pltpu.SMEM),
            pl.BlockSpec(memory_space=pltpu.VMEM),
            pl.BlockSpec(memory_space=pltpu.VMEM),
        ],
        out_specs=pl.BlockSpec(memory_space=pltpu.VMEM),
        scratch_shapes=[
            pltpu.VMEM((blocks, dim, rows), jnp.bfloat16),
            pltpu.VMEM((blocks, dim, rows), jnp.bfloat16),
            pltpu.VMEM((blocks, rows, dim), jnp.float32),
            pltpu.VMEM((blocks, rows, dim), jnp.float32),
            pltpu.VMEM((tiles, rows, rows), jnp.float32),
            pltpu.VMEM((tiles, rows, rows), jnp.float32),
        ],
        compiler_params=pltpu.CompilerParams(vmem_limit_bytes=40 * 1024 * 1024),
        cost_estimate=pl.CostEstimate(flops=3 * 10**9, bytes_accessed=8 * 2**20, transcendentals=4 * 10**6),
    )(first, ends, x)


def body(queries, keys, values, out_grad, doc_lengths):
    rows, heads, dim = queries.shape
    kv_heads = keys.shape[1]
    group = heads // kv_heads
    blocks = lax.axis_size("ctx")
    docs = doc_lengths.shape[0]
    upto = jnp.arange(docs)[:, None] >= jnp.arange(docs)[None, :]
    ends = jnp.sum(jnp.where(upto, doc_lengths[None, :], 0), axis=1)
    heads_pos = jnp.arange(blocks, dtype=jnp.int32) * rows
    start = jnp.max(jnp.where(ends[None, :] <= heads_pos[:, None], ends[None, :], 0), axis=1)
    first = jnp.maximum(start, heads_pos - (WINDOW - 1)) // rows
    first = jnp.maximum(first, 0).astype(jnp.int32)

    def by_head(array, copies):
        array = jnp.swapaxes(array, 0, 1)
        return jnp.repeat(array, copies, axis=0) if copies > 1 else array

    packed = jnp.stack(
        (by_head(queries, 1), by_head(out_grad, 1), by_head(keys, group), by_head(values, group)), 1
    )
    x = lax.all_to_all(packed, "ctx", 0, 0)
    y = attention(first, ends[:, None].astype(jnp.int32), x)
    back = lax.all_to_all(y, "ctx", 0, 0)
    attended = jnp.swapaxes(back[:, 0], 0, 1)
    query_grad = jnp.swapaxes(back[:, 1], 0, 1)
    kv = back[:, 2:].astype(jnp.float32).reshape(kv_heads, group, 2, rows, dim).sum(1)
    kv = jnp.swapaxes(kv, 0, 2).astype(jnp.bfloat16)
    return attended, query_grad, kv[:, 0], kv[:, 1]


def solution(mesh):
    spec = P(("dp", "ctx"), "head", None)
    return jax.shard_map(
        body,
        mesh=mesh,
        in_specs=(spec, spec, spec, spec, P("dp")),
        out_specs=(spec, spec, spec, spec),
        check_vma=False,
    )
```

```python
import functools

import jax
import jax.numpy as jnp
from jax import lax
from jax.experimental import pallas as pl
from jax.experimental.pallas import tpu as pltpu
from jax.sharding import PartitionSpec as P

WINDOW = 1024
SCALING = 168.0 ** (-0.5)
LOG2E = 1.4426950408889634
NEG = -1e30

NT = (((1,), (1,)), ((), ()))
NN = (((1,), (0,)), ((), ()))


def dot(a, b, dims):
    return lax.dot_general(a, b, dims, preferred_element_type=jnp.float32)


def attention_kernel(
    meta_ref, ends_ref, kv_ref, halo_ref, x_ref, y_ref, dkv_ref, dhalo_ref, k_ref, kt_ref, acc_ref, s_ref, g_ref,
    *, blocks, reach_back, rows, group,
):
    dim = x_ref.shape[3]
    wide = group * rows

    def halo_step(t, carry):
        for n in range(2):
            tile = halo_ref[t, n]
            k_ref[t, n] = tile
            kt_ref[t, n] = tile.T
            acc_ref[t, n] = jnp.zeros((rows, dim), jnp.float32)
        return carry

    def copy_step(t, carry):
        for n in range(2):
            tile = kv_ref[t, n]
            k_ref[reach_back + t, n] = tile
            kt_ref[reach_back + t, n] = tile.T
        return carry

    lax.fori_loop(0, reach_back, halo_step, 0)
    lax.fori_loop(0, blocks, copy_step, 0, unroll=2)

    lane = lax.rem(lax.broadcasted_iota(jnp.int32, (1, wide), 1), rows)
    diff = lane - lax.broadcasted_iota(jnp.int32, (rows, wide), 0)

    def query_tile(i, count):
        own = i + reach_back
        first = own - (count - 1)
        q = x_ref[i, 0:group].reshape(wide, dim)
        do = x_ref[i, group:2 * group].reshape(wide, dim)
        pos = meta_ref[blocks] + i * rows + lane
        ends = ends_ref[...]
        start = jnp.max(jnp.where(ends <= pos, ends, 0), axis=0, keepdims=True)
        reach = pos - jnp.maximum(start, pos - (WINDOW - 1))
        top = None
        for t in range(count):
            raw = dot(k_ref[first + t, 0], q, NT)
            offset = (count - 1 - t) * rows
            keep = diff <= reach - offset
            if offset == 0:
                keep = keep & (diff >= 0)
            raw = jnp.where(keep, raw, NEG)
            s_ref[t] = raw
            here = jnp.max(raw, axis=0, keepdims=True)
            top = here if top is None else jnp.maximum(top, here)
            g_ref[t] = dot(k_ref[first + t, 1], do, NT)
        total = mixed = 0.0
        for t in range(count):
            p = jnp.exp2((s_ref[t] - top) * (SCALING * LOG2E))
            s_ref[t] = p
            total += jnp.sum(p, axis=0, keepdims=True)
            mixed += jnp.sum(p * g_ref[t], axis=0, keepdims=True)
        inverse = 1.0 / total
        row_total = mixed * inverse
        out = dq = 0.0
        for t in range(count):
            w = s_ref[t] * inverse
            wb = w.astype(jnp.bfloat16)
            ds = (w * (g_ref[t] - row_total)).astype(jnp.bfloat16)
            out += dot(kt_ref[first + t, 1], wb, NN)
            dq += dot(kt_ref[first + t, 0], ds, NN)
            if t == count - 1:
                acc_ref[own, 1] = dot(wb, do, NN)
                acc_ref[own, 0] = dot(ds, q, NN)
            else:
                acc_ref[first + t, 1] += dot(wb, do, NN)
                acc_ref[first + t, 0] += dot(ds, q, NN)
        for n in range(group):
            y_ref[i, n] = out[:, n * rows:(n + 1) * rows].T.astype(jnp.bfloat16)
            y_ref[i, group + n] = (SCALING * dq[:, n * rows:(n + 1) * rows]).T.astype(jnp.bfloat16)

    def query_step(i, carry):
        count = meta_ref[i]
        for n in range(1, reach_back + 2):
            pl.when(count == n)(functools.partial(query_tile, i, n))
        return carry

    lax.fori_loop(0, blocks, query_step, 0)

    for t in range(reach_back):
        dhalo_ref[t, 0] = (SCALING * acc_ref[t, 0]).astype(jnp.bfloat16)
        dhalo_ref[t, 1] = acc_ref[t, 1].astype(jnp.bfloat16)

    def write_step(t, carry):
        dkv_ref[t, 0] = SCALING * acc_ref[reach_back + t, 0]
        dkv_ref[t, 1] = acc_ref[reach_back + t, 1]
        return carry

    lax.fori_loop(0, blocks, write_step, 0, unroll=2)


def attention(meta, ends, kv, halo, x):
    blocks, _, rows, dim = kv.shape
    reach_back = halo.shape[0]
    group = x.shape[1] // 2
    vmem = pl.BlockSpec(memory_space=pltpu.VMEM)
    return pl.pallas_call(
        functools.partial(attention_kernel, blocks=blocks, reach_back=reach_back, rows=rows, group=group),
        out_shape=(
            jax.ShapeDtypeStruct(x.shape, jnp.bfloat16),
            jax.ShapeDtypeStruct(kv.shape, jnp.float32),
            jax.ShapeDtypeStruct(halo.shape, jnp.bfloat16),
        ),
        in_specs=[pl.BlockSpec(memory_space=pltpu.SMEM), vmem, vmem, vmem, vmem],
        out_specs=(vmem, vmem, vmem),
        scratch_shapes=[
            pltpu.VMEM((reach_back + blocks, 2, rows, dim), jnp.bfloat16),
            pltpu.VMEM((reach_back + blocks, 2, dim, rows), jnp.bfloat16),
            pltpu.VMEM((reach_back + blocks, 2, rows, dim), jnp.float32),
            pltpu.VMEM((reach_back + 1, rows, group * rows), jnp.float32),
            pltpu.VMEM((reach_back + 1, rows, group * rows), jnp.float32),
        ],
        compiler_params=pltpu.CompilerParams(vmem_limit_bytes=40 * 1024 * 1024),
        cost_estimate=pl.CostEstimate(flops=5 * 10**9, bytes_accessed=8 * 2**20, transcendentals=4 * 10**6),
    )(meta, ends, kv, halo, x)


def body(queries, keys, values, out_grad, doc_lengths):
    rows, heads, dim = queries.shape
    kv_heads = keys.shape[1]
    group = heads // kv_heads
    devices = lax.axis_size("ctx")
    parts = devices // kv_heads
    reach_back = WINDOW // rows
    where = lax.axis_index("ctx") // kv_heads
    groups = [[p * kv_heads + j for j in range(kv_heads)] for p in range(parts)]
    onward = [(p * kv_heads + j, (p + 1) * kv_heads + j) for p in range(parts - 1) for j in range(kv_heads)]

    docs = doc_lengths.shape[0]
    upto = jnp.arange(docs)[:, None] >= jnp.arange(docs)[None, :]
    ends = jnp.sum(jnp.where(upto, doc_lengths[None, :], 0), axis=1)
    tile = where * kv_heads + jnp.arange(kv_heads, dtype=jnp.int32)
    start = jnp.max(jnp.where(ends[None, :] <= tile[:, None] * rows, ends[None, :], 0), axis=1)
    first = jnp.maximum(start, tile * rows - (WINDOW - 1))
    count = tile - jnp.maximum(first, 0) // rows + 1
    meta = jnp.concatenate((count, (where * kv_heads * rows)[None])).astype(jnp.int32)

    def exchange(array):
        return lax.all_to_all(array, "ctx", 0, 0, axis_index_groups=groups)

    kv = exchange(jnp.stack((jnp.swapaxes(keys, 0, 1), jnp.swapaxes(values, 0, 1)), 1))
    halo = lax.ppermute(kv[kv_heads - reach_back:], "ctx", onward)
    x = jnp.concatenate(
        [jnp.swapaxes(a, 0, 1).reshape(kv_heads, group, rows, dim) for a in (queries, out_grad)], 1
    )
    x = exchange(x)
    y, dkv, dhalo = attention(meta, ends[:, None].astype(jnp.int32), kv, halo, x)
    dhalo = lax.ppermute(dhalo, "ctx", [(b, a) for a, b in onward])
    y = exchange(y)
    still = kv_heads - reach_back
    dkv = jnp.concatenate((dkv[:still], dkv[still:] + dhalo.astype(jnp.float32)), 0).astype(jnp.bfloat16)
    dkv = exchange(dkv)
    attended = jnp.swapaxes(y[:, :group].reshape(heads, rows, dim), 0, 1)
    query_grad = jnp.swapaxes(y[:, group:].reshape(heads, rows, dim), 0, 1)
    return attended, query_grad, jnp.swapaxes(dkv[:, 0], 0, 1), jnp.swapaxes(dkv[:, 1], 0, 1)


def solution(mesh):
    spec = P(("dp", "ctx"), "head", None)
    return jax.shard_map(
        body,
        mesh=mesh,
        in_specs=(spec, spec, spec, spec, P("dp")),
        out_specs=(spec, spec, spec, spec),
        check_vma=False,
    )
```

```python
import functools

import jax
import jax.numpy as jnp
from jax import lax
from jax.experimental import pallas as pl
from jax.experimental.pallas import tpu as pltpu
from jax.sharding import PartitionSpec as P

WINDOW = 1024
SCALING = 168.0 ** (-0.5)
LOG2E = 1.4426950408889634
NEG = -1e30
PIECES = 2

NT = (((1,), (1,)), ((), ()))
NN = (((1,), (0,)), ((), ()))

VMEM = pl.BlockSpec(memory_space=pltpu.VMEM)
SMEM = pl.BlockSpec(memory_space=pltpu.SMEM)


def dot(a, b, dims):
    return lax.dot_general(a, b, dims, preferred_element_type=jnp.float32)


def place(i, turn, blocks):
    return lax.rem(i + turn, blocks)


def prepare_kernel(meta_ref, kv_ref, halo_ref, k_ref, kt_ref, *, blocks, tile):
    before = halo_ref.shape[0]
    cuts = kv_ref.shape[2] // tile
    turn = meta_ref[blocks + 1]

    def put(source, index, at):
        for n in range(2):
            for c in range(cuts):
                part = source[index, n, c * tile:(c + 1) * tile]
                k_ref[at * cuts + c, n] = part
                kt_ref[at * cuts + c, n] = part.T

    def halo_step(t, carry):
        put(halo_ref, t, t)
        return carry

    def own_step(t, carry):
        put(kv_ref, place(t, turn, blocks), before + t)
        return carry

    lax.fori_loop(0, before, halo_step, 0)
    lax.fori_loop(0, blocks, own_step, 0, unroll=2)


def prepare(meta, kv, halo, tile):
    blocks, _, rows, dim = kv.shape
    tiles = (halo.shape[0] + blocks) * (rows // tile)
    return pl.pallas_call(
        functools.partial(prepare_kernel, blocks=blocks, tile=tile),
        out_shape=(
            jax.ShapeDtypeStruct((tiles, 2, tile, dim), kv.dtype),
            jax.ShapeDtypeStruct((tiles, 2, dim, tile), kv.dtype),
        ),
        in_specs=[SMEM, VMEM, VMEM],
        out_specs=(VMEM, VMEM),
        compiler_params=pltpu.CompilerParams(vmem_limit_bytes=12 * 1024 * 1024),
        cost_estimate=pl.CostEstimate(flops=10**6, bytes_accessed=6 * 2**20, transcendentals=0),
    )(meta, kv, halo)


def attention_kernel(*refs, blocks, before, group, piece, first_piece, last_piece):
    refs = list(refs)
    meta_ref, ends_ref, k_ref, kt_ref, x_ref = refs[:5]
    refs = refs[5:]
    if not first_piece:
        given_ref = refs.pop(0)
    y_ref = refs.pop(0)
    if last_piece:
        dkv_ref, dhalo_ref, acc_ref, s_ref, g_ref = refs
    else:
        acc_ref, s_ref, g_ref = refs
    tile, dim = x_ref.shape[2:]
    wide = group * tile
    tiles = k_ref.shape[0]
    cuts = tiles // (blocks + before)
    base, turn = meta_ref[blocks], meta_ref[blocks + 1]

    def start_step(t, carry):
        if first_piece:
            acc_ref[t] = jnp.zeros(acc_ref.shape[1:], jnp.float32)
        else:
            acc_ref[t] = given_ref[t]
        return carry

    lax.fori_loop(0, tiles, start_step, 0, unroll=4)

    lane = lax.rem(lax.broadcasted_iota(jnp.int32, (1, wide), 1), tile)
    diff = lane - lax.broadcasted_iota(jnp.int32, (2 * tile, wide), 0)

    def query_tile(i, count):
        own = (i + before) * cuts + piece
        first = own - (count - 1)
        at = place(i, turn, blocks)
        q = x_ref[at, 0:group].reshape(wide, dim)
        do = x_ref[at, group:2 * group].reshape(wide, dim)
        pos = base + (i * cuts + piece) * tile + lane
        ends = ends_ref[...]
        start = jnp.max(jnp.where(ends <= pos, ends, 0), axis=0, keepdims=True)
        reach = pos - jnp.maximum(start, pos - (WINDOW - 1))
        chunks = [(0, 1)] * (count % 2) + [(a, 2) for a in range(count % 2, count, 2)]
        top = None
        for a, n in chunks:
            raw = dot(k_ref[pl.ds(first + a, n), 0].reshape(n * tile, dim), q, NT)
            offset = (count - 1 - a) * tile
            keep = diff[:n * tile] <= reach - offset
            if a + n == count:
                keep = keep & (diff[:n * tile] >= -offset)
            raw = jnp.where(keep, raw, NEG)
            s_ref[a * tile:(a + n) * tile] = raw
            here = jnp.max(raw, axis=0, keepdims=True)
            top = here if top is None else jnp.maximum(top, here)
            g_ref[a * tile:(a + n) * tile] = dot(k_ref[pl.ds(first + a, n), 1].reshape(n * tile, dim), do, NT)
        total = mixed = 0.0
        for a, n in chunks:
            p = jnp.exp2((s_ref[a * tile:(a + n) * tile] - top) * (SCALING * LOG2E))
            s_ref[a * tile:(a + n) * tile] = p
            total += jnp.sum(p, axis=0, keepdims=True)
            mixed += jnp.sum(p * g_ref[a * tile:(a + n) * tile], axis=0, keepdims=True)
        inverse = 1.0 / total
        row_total = mixed * inverse
        out = dq = 0.0
        for a, n in chunks:
            w = s_ref[a * tile:(a + n) * tile] * inverse
            wb = w.astype(jnp.bfloat16)
            ds = (w * (g_ref[a * tile:(a + n) * tile] - row_total)).astype(jnp.bfloat16)
            kt, vt = (
                jnp.concatenate([kt_ref[first + a + c, m] for c in range(n)], axis=1) for m in range(2)
            )
            out += dot(vt, wb, NN)
            dq += dot(kt, ds, NN)
            acc_ref[pl.ds(first + a, n), 1] += dot(wb, do, NN).reshape(n, tile, dim)
            acc_ref[pl.ds(first + a, n), 0] += dot(ds, q, NN).reshape(n, tile, dim)
        for n in range(group):
            y_ref[at, n] = out[:, n * tile:(n + 1) * tile].T.astype(jnp.bfloat16)
            y_ref[at, group + n] = (SCALING * dq[:, n * tile:(n + 1) * tile]).T.astype(jnp.bfloat16)

    def query_step(i, carry):
        count = meta_ref[i]
        for n in range(1, before * cuts + 2):
            pl.when(count == n)(functools.partial(query_tile, i, n))
        return carry

    lax.fori_loop(0, blocks, query_step, 0)

    if last_piece:
        def result(t, c):
            return SCALING * acc_ref[t * cuts + c, 0], acc_ref[t * cuts + c, 1]

        def halo_step(t, carry):
            for c in range(cuts):
                for n, value in enumerate(result(t, c)):
                    dhalo_ref[t, n * cuts + c] = value.astype(jnp.bfloat16)
            return carry

        def own_step(t, carry):
            for c in range(cuts):
                for n, value in enumerate(result(before + t, c)):
                    dkv_ref[place(t, turn, blocks), n * cuts + c] = value
            return carry

        lax.fori_loop(0, before, halo_step, 0)
        lax.fori_loop(0, blocks, own_step, 0, unroll=2)


def attention(meta, ends, k, kt, x, given, before, piece):
    blocks, _, tile, dim = x.shape
    group = x.shape[1] // 2
    tiles = k.shape[0]
    cuts = tiles // (blocks + before)
    first_piece, last_piece = given is None, piece == PIECES - 1
    acc = jax.ShapeDtypeStruct((tiles, 2, tile, dim), jnp.float32)
    outs = [jax.ShapeDtypeStruct(x.shape, jnp.bfloat16)]
    scratch = [pltpu.VMEM(((before * cuts + 1) * tile, group * tile), jnp.float32)] * 2
    if last_piece:
        outs += [
            jax.ShapeDtypeStruct((blocks, 2 * cuts, tile, dim), jnp.float32),
            jax.ShapeDtypeStruct((before, 2 * cuts, tile, dim), jnp.bfloat16),
        ]
        scratch = [pltpu.VMEM(acc.shape, acc.dtype)] + scratch
    else:
        outs.append(acc)
    operands = [meta, ends, k, kt, x] + ([] if first_piece else [given])
    return pl.pallas_call(
        functools.partial(
            attention_kernel, blocks=blocks, before=before, group=group, piece=piece,
            first_piece=first_piece, last_piece=last_piece,
        ),
        out_shape=tuple(outs),
        in_specs=[SMEM] + [VMEM] * (len(operands) - 1),
        out_specs=(VMEM,) * len(outs),
        scratch_shapes=scratch,
        compiler_params=pltpu.CompilerParams(vmem_limit_bytes=20 * 1024 * 1024),
        cost_estimate=pl.CostEstimate(flops=3 * 10**9, bytes_accessed=12 * 2**20, transcendentals=2 * 10**6),
    )(*operands)


def after(array, other):
    return lax.optimization_barrier((array, other))[0]


def body(queries, keys, values, out_grad, doc_lengths):
    rows, heads, dim = queries.shape
    kv_heads = keys.shape[1]
    group = heads // kv_heads
    blocks = kv_heads
    parts = lax.axis_size("ctx") // blocks
    before = WINDOW // rows
    tile = rows // PIECES
    turns = [(p % 2) * (blocks // 2) for p in range(parts)]
    groups = [[p * blocks + (r + turns[p]) % blocks for r in range(blocks)] for p in range(parts)]
    onward = [(groups[p][r], groups[p + 1][r]) for p in range(parts - 1) for r in range(blocks)]
    part = lax.axis_index("ctx") // blocks

    docs = doc_lengths.shape[0]
    upto = jnp.arange(docs)[:, None] >= jnp.arange(docs)[None, :]
    ends = jnp.sum(jnp.where(upto, doc_lengths[None, :], 0), axis=1)
    base = part * blocks * rows
    turn = lax.rem(part, 2) * (blocks // 2)
    metas = []
    for piece in range(PIECES):
        position = base + jnp.arange(blocks, dtype=jnp.int32) * rows + piece * tile
        start = jnp.max(jnp.where(ends[None, :] <= position[:, None], ends[None, :], 0), axis=1)
        first = jnp.maximum(jnp.maximum(start, position - (WINDOW - 1)), 0)
        metas.append(jnp.concatenate((position // tile - first // tile + 1, jnp.stack((base, turn)))).astype(jnp.int32))
    ends = ends[:, None].astype(jnp.int32)

    def exchange(array):
        return lax.all_to_all(array, "ctx", 0, 0, axis_index_groups=groups)

    def by_head(array):
        array = jnp.swapaxes(array, 0, 1)
        return array.reshape(kv_heads, array.shape[0] // kv_heads, array.shape[1], dim)

    def by_token(array):
        array = array.reshape(array.shape[0] * array.shape[1], array.shape[2], dim)
        return jnp.swapaxes(array, 0, 1)

    kv = exchange(jnp.concatenate((by_head(keys), by_head(values)), 1))
    tail = jnp.stack([kv[(blocks - before + t + turns[0]) % blocks] for t in range(before)]) if turns[0] else kv[blocks - before:]
    halo = lax.ppermute(tail, "ctx", onward)
    packed = [
        jnp.concatenate([by_head(a[p * tile:(p + 1) * tile]) for a in (queries, out_grad)], 1) for p in range(PIECES)
    ]
    x0 = exchange(after(packed[0], kv))
    k, kt = prepare(metas[0], kv, halo, tile)
    x1 = exchange(after(packed[1], x0))
    y0, acc = attention(metas[0], ends, k, kt, x0, None, before, 0)
    y1, dkv, dhalo = attention(metas[1], ends, k, kt, x1, acc, before, 1)
    dhalo = lax.ppermute(dhalo, "ctx", [(b, a) for a, b in onward])
    y0 = exchange(after(y0, x1))
    still = blocks - before
    dkv = jnp.concatenate((dkv[:still], dkv[still:] + dhalo.astype(jnp.float32)), 0).astype(jnp.bfloat16)
    last = exchange(after(jnp.concatenate((y1, dkv), 1), y0))
    y1, dk, dv = last[:, :2 * group], last[:, 2 * group:2 * group + PIECES], last[:, 2 * group + PIECES:]
    attended = jnp.concatenate([by_token(y[:, :group]) for y in (y0, y1)], 0)
    query_grad = jnp.concatenate([by_token(y[:, group:]) for y in (y0, y1)], 0)
    dk, dv = (jnp.swapaxes(a.reshape(kv_heads, rows, dim), 0, 1) for a in (dk, dv))
    return attended, query_grad, dk, dv


def solution(mesh):
    spec = P(("dp", "ctx"), "head", None)
    return jax.shard_map(
        body,
        mesh=mesh,
        in_specs=(spec, spec, spec, spec, P("dp")),
        out_specs=(spec, spec, spec, spec),
        check_vma=False,
    )
```

```python
import functools

import jax
import jax.numpy as jnp
from jax import lax
from jax.experimental import pallas as pl
from jax.experimental.pallas import tpu as pltpu
from jax.sharding import PartitionSpec as P

WINDOW = 1024
SCALING = 168.0 ** (-0.5)
LOG2E = 1.4426950408889634
NEG = -1e30
CUTS = (192, 64)
TILE = 128

NT = (((1,), (1,)), ((), ()))
NN = (((1,), (0,)), ((), ()))

VMEM = pl.BlockSpec(memory_space=pltpu.VMEM)
SMEM = pl.BlockSpec(memory_space=pltpu.SMEM)


def dot(a, b, dims):
    return lax.dot_general(a, b, dims, preferred_element_type=jnp.float32)


def place(i, turn, blocks):
    return lax.rem(i + turn, blocks)


def prepare_kernel(meta_ref, kv_ref, halo_ref, k_ref, kt_ref, *, blocks, tile):
    before = halo_ref.shape[0]
    cuts = kv_ref.shape[2] // tile
    turn = meta_ref[blocks + 1]

    def put(source, index, at):
        for n in range(2):
            for c in range(cuts):
                part = source[index, n, c * tile:(c + 1) * tile]
                k_ref[at * cuts + c, n] = part
                kt_ref[at * cuts + c, n] = part.T

    def halo_step(t, carry):
        put(halo_ref, t, t)
        return carry

    def own_step(t, carry):
        put(kv_ref, place(t, turn, blocks), before + t)
        return carry

    lax.fori_loop(0, before, halo_step, 0)
    lax.fori_loop(0, blocks, own_step, 0, unroll=2)


def prepare(meta, kv, halo, tile):
    blocks, _, rows, dim = kv.shape
    tiles = (halo.shape[0] + blocks) * (rows // tile)
    return pl.pallas_call(
        functools.partial(prepare_kernel, blocks=blocks, tile=tile),
        out_shape=(
            jax.ShapeDtypeStruct((tiles, 2, tile, dim), kv.dtype),
            jax.ShapeDtypeStruct((tiles, 2, dim, tile), kv.dtype),
        ),
        in_specs=[SMEM, VMEM, VMEM],
        out_specs=(VMEM, VMEM),
        compiler_params=pltpu.CompilerParams(vmem_limit_bytes=24 * 1024 * 1024),
        cost_estimate=pl.CostEstimate(flops=10**6, bytes_accessed=6 * 2**20, transcendentals=0),
    )(meta, kv, halo)


def attention_kernel(*refs, blocks, before, group, rows, row0, first_piece, last_piece):
    refs = list(refs)
    meta_ref, ends_ref, k_hbm, kt_hbm, x_ref = refs[:5]
    refs = refs[5:]
    if not first_piece:
        given_hbm = refs.pop(0)
    y_hbm = refs.pop(0)
    if last_piece:
        dkv_ref, dhalo_ref = refs[:2]
        refs = refs[2:]
    else:
        acc_hbm = refs.pop(0)
    k_ref, kt_ref, acc_ref, s_ref, g_ref, y_ref, k_sem, kt_sem, acc_sem, y_sem = refs[:10]
    k_copy = pltpu.make_async_copy(k_hbm, k_ref, k_sem)
    kt_copy = pltpu.make_async_copy(kt_hbm, kt_ref, kt_sem)
    k_copy.start()
    kt_copy.start()
    if not first_piece:
        given_ref = refs[10]
        given_copy = pltpu.make_async_copy(given_hbm, given_ref, acc_sem)
        given_copy.start()
    part, dim = x_ref.shape[2:]
    tile = k_ref.shape[2]
    wide = group * part
    tiles = k_ref.shape[0]
    cuts = rows // tile
    final = (row0 + part - 1) // tile
    base, turn = meta_ref[blocks], meta_ref[blocks + 1]

    def start_step(t, carry):
        acc_ref[t] = jnp.zeros(acc_ref.shape[1:], jnp.float32)
        return carry

    lax.fori_loop(0, tiles, start_step, 0, unroll=4)

    lane = lax.rem(lax.broadcasted_iota(jnp.int32, (1, wide), 1), part)
    diff = lane - lax.broadcasted_iota(jnp.int32, (2 * tile, wide), 0)
    k_copy.wait()
    kt_copy.wait()

    def y_copy(at):
        return pltpu.make_async_copy(y_ref.at[at], y_hbm.at[at], y_sem.at[at])

    def query_tile(i, count):
        first = (i + before) * cuts + final - (count - 1)
        at = place(i, turn, blocks)
        q = x_ref[at, 0:group].reshape(wide, dim)
        do = x_ref[at, group:2 * group].reshape(wide, dim)
        pos = base + i * rows + row0 + lane
        ends = ends_ref[...]
        start = jnp.max(jnp.where(ends <= pos, ends, 0), axis=0, keepdims=True)
        reach = pos - jnp.maximum(start, pos - (WINDOW - 1))
        chunks = [(0, 1)] * (count % 2) + [(a, 2) for a in range(count % 2, count, 2)]
        top = None
        for a, n in chunks:
            raw = dot(k_ref[pl.ds(first + a, n), 0].reshape(n * tile, dim), q, NT)
            offset = row0 - (final - (count - 1) + a) * tile
            keep = diff[:n * tile] <= reach - offset
            if offset < n * tile - 1:
                keep = keep & (diff[:n * tile] >= -offset)
            raw = jnp.where(keep, raw, NEG)
            s_ref[a * tile:(a + n) * tile] = raw
            here = jnp.max(raw, axis=0, keepdims=True)
            top = here if top is None else jnp.maximum(top, here)
            g_ref[a * tile:(a + n) * tile] = dot(k_ref[pl.ds(first + a, n), 1].reshape(n * tile, dim), do, NT)
        total = mixed = 0.0
        for a, n in chunks:
            p = jnp.exp2((s_ref[a * tile:(a + n) * tile] - top) * (SCALING * LOG2E))
            s_ref[a * tile:(a + n) * tile] = p
            total += jnp.sum(p, axis=0, keepdims=True)
            mixed += jnp.sum(p * g_ref[a * tile:(a + n) * tile], axis=0, keepdims=True)
        inverse = 1.0 / total
        row_total = mixed * inverse
        out = dq = 0.0
        for a, n in chunks:
            w = s_ref[a * tile:(a + n) * tile] * inverse
            wb = w.astype(jnp.bfloat16)
            ds = (w * (g_ref[a * tile:(a + n) * tile] - row_total)).astype(jnp.bfloat16)
            kt, vt = (
                jnp.concatenate([kt_ref[first + a + c, m] for c in range(n)], axis=1) for m in range(2)
            )
            out += dot(vt, wb, NN)
            dq += dot(kt, ds, NN)
            acc_ref[pl.ds(first + a, n), 1] += dot(wb, do, NN).reshape(n, tile, dim)
            acc_ref[pl.ds(first + a, n), 0] += dot(ds, q, NN).reshape(n, tile, dim)
        y_ref[at, 0:group] = out.T.astype(jnp.bfloat16).reshape(group, part, dim)
        y_ref[at, group:2 * group] = (SCALING * dq).T.astype(jnp.bfloat16).reshape(group, part, dim)

    def query_step(i, carry):
        count = meta_ref[i]
        most = final + 1 + (before * rows - row0 - 1) // tile + 1
        for n in range(1, most + 1):
            pl.when(count == n)(functools.partial(query_tile, i, n))
        y_copy(place(i, turn, blocks)).start()
        return carry

    lax.fori_loop(0, blocks, query_step, 0)

    if last_piece:
        given_copy.wait()

        def result(t, c):
            both = acc_ref[t * cuts + c] + given_ref[t * cuts + c]
            return SCALING * both[0], both[1]

        def halo_step(t, carry):
            for c in range(cuts):
                for n, value in enumerate(result(t, c)):
                    dhalo_ref[t, n, c * tile:(c + 1) * tile] = value.astype(jnp.bfloat16)
            return carry

        def own_step(t, carry):
            for c in range(cuts):
                for n, value in enumerate(result(before + t, c)):
                    dkv_ref[place(t, turn, blocks), n, c * tile:(c + 1) * tile] = value
            return carry

        lax.fori_loop(0, before, halo_step, 0)
        lax.fori_loop(0, blocks, own_step, 0, unroll=2)
    else:
        acc_copy = pltpu.make_async_copy(acc_ref, acc_hbm, acc_sem)
        acc_copy.start()
        acc_copy.wait()

    def wait_step(i, carry):
        y_copy(i).wait()
        return carry

    lax.fori_loop(0, blocks, wait_step, 0)


def attention(meta, ends, k, kt, x, given, before, rows, row0):
    blocks, _, part, dim = x.shape
    group = x.shape[1] // 2
    tiles, _, tile, _ = k.shape
    first_piece, last_piece = given is None, row0 + part == rows
    hbm = pl.BlockSpec(memory_space=pl.ANY)
    acc = jax.ShapeDtypeStruct((tiles, 2, tile, dim), jnp.float32)
    outs = [jax.ShapeDtypeStruct(x.shape, jnp.bfloat16)]
    most = (row0 + part - 1) // tile + 2 + (before * rows - row0 - 1) // tile
    scratch = [
        pltpu.VMEM(k.shape, k.dtype),
        pltpu.VMEM(kt.shape, kt.dtype),
        pltpu.VMEM(acc.shape, acc.dtype),
        pltpu.VMEM((most * tile, group * part), jnp.float32),
        pltpu.VMEM((most * tile, group * part), jnp.float32),
        pltpu.VMEM(x.shape, jnp.bfloat16),
        pltpu.SemaphoreType.DMA,
        pltpu.SemaphoreType.DMA,
        pltpu.SemaphoreType.DMA,
        pltpu.SemaphoreType.DMA((blocks,)),
    ]
    if last_piece:
        outs += [
            jax.ShapeDtypeStruct((blocks, 2, rows, dim), jnp.float32),
            jax.ShapeDtypeStruct((before, 2, rows, dim), jnp.bfloat16),
        ]
        scratch.append(pltpu.VMEM(acc.shape, acc.dtype))
    else:
        outs.append(acc)
    operands = [meta, ends, k, kt, x] + ([] if first_piece else [given])
    return pl.pallas_call(
        functools.partial(
            attention_kernel, blocks=blocks, before=before, group=group, rows=rows, row0=row0,
            first_piece=first_piece, last_piece=last_piece,
        ),
        out_shape=tuple(outs),
        in_specs=[SMEM, VMEM, hbm, hbm, VMEM] + [hbm] * (not first_piece),
        out_specs=(hbm, VMEM, VMEM) if last_piece else (hbm, hbm),
        scratch_shapes=scratch,
        compiler_params=pltpu.CompilerParams(vmem_limit_bytes=60 * 1024 * 1024),
        cost_estimate=pl.CostEstimate(flops=3 * 10**9, bytes_accessed=12 * 2**20, transcendentals=2 * 10**6),
    )(*operands)


def combine_kernel(y_ref, dkv_ref, dhalo_ref, out_ref, *, blocks, before, slots):
    count = y_ref.shape[1]
    out_ref[0, 0:count] = y_ref[0]
    behind = pl.program_id(0) >= blocks - before
    for n in range(2):
        value = dkv_ref[0, n] + jnp.where(behind, dhalo_ref[0, n].astype(jnp.float32), 0.0)
        out_ref[0, count + n * slots:count + (n + 1) * slots] = value.astype(out_ref.dtype).reshape(
            slots, y_ref.shape[2], y_ref.shape[3]
        )


def combine(y, dkv, dhalo):
    blocks, count, part, dim = y.shape
    rows, before = dkv.shape[2], dhalo.shape[0]
    slots = rows // part
    return pl.pallas_call(
        functools.partial(combine_kernel, blocks=blocks, before=before, slots=slots),
        grid=(blocks,),
        out_shape=jax.ShapeDtypeStruct((blocks, count + 2 * slots, part, dim), y.dtype),
        in_specs=[
            pl.BlockSpec((1, count, part, dim), lambda i: (i, 0, 0, 0)),
            pl.BlockSpec((1, 2, rows, dim), lambda i: (i, 0, 0, 0)),
            pl.BlockSpec((1, 2, rows, dim), lambda i: (jnp.maximum(i - (blocks - before), 0), 0, 0, 0)),
        ],
        out_specs=pl.BlockSpec((1, count + 2 * slots, part, dim), lambda i: (i, 0, 0, 0)),
        compiler_params=pltpu.CompilerParams(vmem_limit_bytes=60 * 1024 * 1024),
        cost_estimate=pl.CostEstimate(flops=10**6, bytes_accessed=6 * 2**20, transcendentals=0),
    )(y, dkv, dhalo)


def after(array, other):
    return lax.optimization_barrier((array, other))[0]


def body(queries, keys, values, out_grad, doc_lengths):
    rows, heads, dim = queries.shape
    kv_heads = keys.shape[1]
    group = heads // kv_heads
    blocks = kv_heads
    parts = lax.axis_size("ctx") // blocks
    before = WINDOW // rows
    tile = TILE
    starts = [sum(CUTS[:p]) for p in range(len(CUTS))]
    turns = [(p % 2) * (blocks // 2) for p in range(parts)]
    groups = [[p * blocks + (r + turns[p]) % blocks for r in range(blocks)] for p in range(parts)]
    onward = [(groups[p][r], groups[p + 1][r]) for p in range(parts - 1) for r in range(blocks)]
    part = lax.axis_index("ctx") // blocks

    docs = doc_lengths.shape[0]
    upto = jnp.arange(docs)[:, None] >= jnp.arange(docs)[None, :]
    ends = jnp.sum(jnp.where(upto, doc_lengths[None, :], 0), axis=1)
    base = part * blocks * rows
    turn = lax.rem(part, 2) * (blocks // 2)
    metas = []
    for row0, part_rows in zip(starts, CUTS):
        position = base + jnp.arange(blocks, dtype=jnp.int32) * rows + row0
        start = jnp.max(jnp.where(ends[None, :] <= position[:, None], ends[None, :], 0), axis=1)
        first = jnp.maximum(jnp.maximum(start, position - (WINDOW - 1)), 0)
        last = (position + part_rows - 1) // tile
        metas.append(jnp.concatenate((last - first // tile + 1, jnp.stack((base, turn)))).astype(jnp.int32))
    ends = ends[:, None].astype(jnp.int32)

    def exchange(array):
        return lax.all_to_all(array, "ctx", 0, 0, axis_index_groups=groups)

    def by_head(array):
        array = jnp.swapaxes(array, 0, 1)
        return array.reshape(kv_heads, array.shape[0] // kv_heads, array.shape[1], dim)

    def by_token(array):
        array = array.reshape(array.shape[0] * array.shape[1], array.shape[2], dim)
        return jnp.swapaxes(array, 0, 1)

    kv = exchange(jnp.concatenate((by_head(keys), by_head(values)), 1))
    tail = jnp.stack([kv[(blocks - before + t + turns[0]) % blocks] for t in range(before)]) if turns[0] else kv[blocks - before:]
    halo = lax.ppermute(tail, "ctx", onward)
    packed = [
        jnp.concatenate([by_head(a[r:r + n]) for a in (queries, out_grad)], 1) for r, n in zip(starts, CUTS)
    ]
    x0 = exchange(after(packed[0], (kv, packed[1])))
    k, kt = prepare(metas[0], kv, halo, tile)
    x1 = exchange(after(packed[1], (x0, k)))
    y0, acc = attention(metas[0], ends, k, kt, x0, None, before, rows, starts[0])
    y1, dkv, dhalo = attention(metas[1], ends, k, kt, x1, acc, before, rows, starts[1])
    dhalo = lax.ppermute(dhalo, "ctx", [(b, a) for a, b in onward])
    y0 = exchange(after(y0, x1))
    last = exchange(after(combine(y1, dkv, dhalo), y0))
    slots = rows // CUTS[1]
    y1, dk, dv = last[:, :2 * group], last[:, 2 * group:2 * group + slots], last[:, 2 * group + slots:]
    attended = jnp.concatenate([by_token(y[:, :group]) for y in (y0, y1)], 0)
    query_grad = jnp.concatenate([by_token(y[:, group:]) for y in (y0, y1)], 0)
    dk, dv = (jnp.swapaxes(a.reshape(kv_heads, rows, dim), 0, 1) for a in (dk, dv))
    return attended, query_grad, dk, dv


def solution(mesh):
    spec = P(("dp", "ctx"), "head", None)
    return jax.shard_map(
        body,
        mesh=mesh,
        in_specs=(spec, spec, spec, spec, P("dp")),
        out_specs=(spec, spec, spec, spec),
        check_vma=False,
    )
```

```python
import functools

import jax
import jax.numpy as jnp
from jax import lax
from jax.experimental import pallas as pl
from jax.experimental.pallas import tpu as pltpu
from jax.sharding import PartitionSpec as P

WINDOW = 1024
SCALING = 168.0 ** (-0.5)
LOG2E = 1.4426950408889634
NEG = -1e30
TILE = 128
VMEM_LIMIT = 48 * 1024 * 1024

NT = (((1,), (1,)), ((), ()))
NN = (((1,), (0,)), ((), ()))

VMEM = pl.BlockSpec(memory_space=pltpu.VMEM)
SMEM = pl.BlockSpec(memory_space=pltpu.SMEM)


def dot(a, b, dims):
    return lax.dot_general(a, b, dims, preferred_element_type=jnp.float32)


def place(i, turn, blocks):
    return lax.rem(i + turn, blocks)


def prepare_kernel(meta_ref, kv_ref, halo_ref, k_ref, kt_ref, *, blocks, tile):
    before = halo_ref.shape[0]
    cuts = kv_ref.shape[2] // tile
    turn = meta_ref[1]

    def put(source, index, at):
        for n in range(2):
            for c in range(cuts):
                part = source[index, n, c * tile:(c + 1) * tile]
                k_ref[at * cuts + c, n] = part
                kt_ref[at * cuts + c, n] = part.T

    def halo_step(t, carry):
        put(halo_ref, t, t)
        return carry

    def own_step(t, carry):
        put(kv_ref, place(t, turn, blocks), before + t)
        return carry

    lax.fori_loop(0, before, halo_step, 0)
    lax.fori_loop(0, blocks, own_step, 0, unroll=2)


def prepare(meta, kv, halo, tile):
    blocks, _, rows, dim = kv.shape
    tiles = (halo.shape[0] + blocks) * (rows // tile)
    return pl.pallas_call(
        functools.partial(prepare_kernel, blocks=blocks, tile=tile),
        out_shape=(
            jax.ShapeDtypeStruct((tiles, 2, tile, dim), kv.dtype),
            jax.ShapeDtypeStruct((tiles, 2, dim, tile), kv.dtype),
        ),
        in_specs=[SMEM, VMEM, VMEM],
        out_specs=(VMEM, VMEM),
        compiler_params=pltpu.CompilerParams(vmem_limit_bytes=24 * 1024 * 1024),
        cost_estimate=pl.CostEstimate(flops=10**6, bytes_accessed=6 * 2**20, transcendentals=0),
    )(meta, kv, halo)


def attention_kernel(
    meta_ref, ends_ref, k_hbm, kt_hbm, x_ref, y_hbm, dkv_ref, dhalo_ref,
    k_ref, kt_ref, acc_ref, s_ref, g_ref, y_ref, k_sem, kt_sem, y_sem, *, blocks, before, group,
):
    k_copy = pltpu.make_async_copy(k_hbm, k_ref, k_sem)
    kt_copy = pltpu.make_async_copy(kt_hbm, kt_ref, kt_sem)
    k_copy.start()
    kt_copy.start()
    rows, dim = x_ref.shape[2:]
    tile = k_ref.shape[2]
    wide = group * tile
    cuts = rows // tile
    base, turn = meta_ref[blocks * cuts], meta_ref[blocks * cuts + 1]

    def zero_step(t, carry):
        acc_ref[t] = jnp.zeros(acc_ref.shape[1:], jnp.float32)
        return carry

    lax.fori_loop(0, before * cuts, zero_step, 0, unroll=4)

    lane = lax.rem(lax.broadcasted_iota(jnp.int32, (1, wide), 1), tile)
    diff = lane - lax.broadcasted_iota(jnp.int32, (2 * tile, wide), 0)
    k_copy.wait()
    kt_copy.wait()

    def y_copy(at):
        return pltpu.make_async_copy(y_ref.at[at], y_hbm.at[at], y_sem.at[at])

    def query_tile(i, at, piece, count):
        own = before * cuts + i
        first = own - (count - 1)
        span = pl.ds(piece * tile, tile)
        q = x_ref[at, 0:group, span].reshape(wide, dim)
        do = x_ref[at, group:2 * group, span].reshape(wide, dim)
        pos = base + i * tile + lane
        ends = ends_ref[...]
        start = jnp.max(jnp.where(ends <= pos, ends, 0), axis=0, keepdims=True)
        reach = pos - jnp.maximum(start, pos - (WINDOW - 1))
        chunks = [(0, 1)] * (count % 2) + [(a, 2) for a in range(count % 2, count, 2)]
        top = None
        for a, n in chunks:
            raw = dot(k_ref[pl.ds(first + a, n), 0].reshape(n * tile, dim), q, NT)
            offset = (count - 1 - a) * tile
            keep = diff[:n * tile] <= reach - offset
            if a + n == count:
                keep = keep & (diff[:n * tile] >= -offset)
            raw = jnp.where(keep, raw, NEG)
            s_ref[a * tile:(a + n) * tile] = raw
            here = jnp.max(raw, axis=0, keepdims=True)
            top = here if top is None else jnp.maximum(top, here)
            g_ref[a * tile:(a + n) * tile] = dot(k_ref[pl.ds(first + a, n), 1].reshape(n * tile, dim), do, NT)
        total = mixed = 0.0
        for a, n in chunks:
            p = jnp.exp2((s_ref[a * tile:(a + n) * tile] - top) * (SCALING * LOG2E))
            s_ref[a * tile:(a + n) * tile] = p
            total += jnp.sum(p, axis=0, keepdims=True)
            mixed += jnp.sum(p * g_ref[a * tile:(a + n) * tile], axis=0, keepdims=True)
        inverse = 1.0 / total
        row_total = mixed * inverse
        out = dq = 0.0
        for a, n in chunks:
            w = s_ref[a * tile:(a + n) * tile] * inverse
            wb = w.astype(jnp.bfloat16)
            ds = (w * (g_ref[a * tile:(a + n) * tile] - row_total)).astype(jnp.bfloat16)
            kt, vt = (
                jnp.concatenate([kt_ref[first + a + c, m] for c in range(n)], axis=1) for m in range(2)
            )
            out += dot(vt, wb, NN)
            dq += dot(kt, ds, NN)
            for m, part in enumerate((dot(ds, q, NN), dot(wb, do, NN))):
                for c in range(n):
                    if a + c == count - 1:
                        acc_ref[own, m] = part[c * tile:]
                    else:
                        acc_ref[first + a + c, m] += part[c * tile:(c + 1) * tile]
        y_ref[at, 0:group, span] = out.T.astype(jnp.bfloat16).reshape(group, tile, dim)
        y_ref[at, group:2 * group, span] = (SCALING * dq).T.astype(jnp.bfloat16).reshape(group, tile, dim)

    def query_step(i, carry):
        block, piece = i // cuts, lax.rem(i, cuts)
        at = place(block, turn, blocks)
        count = meta_ref[i]
        for n in range(1, before * cuts + 2):
            pl.when(count == n)(functools.partial(query_tile, i, at, piece, n))

        @pl.when(piece == cuts - 1)
        def _():
            y_copy(at).start()

        return carry

    lax.fori_loop(0, blocks * cuts, query_step, 0)

    def result(t, c):
        return SCALING * acc_ref[t * cuts + c, 0], acc_ref[t * cuts + c, 1]

    def halo_step(t, carry):
        for c in range(cuts):
            for n, value in enumerate(result(t, c)):
                dhalo_ref[t, n, c * tile:(c + 1) * tile] = value.astype(jnp.bfloat16)
        return carry

    def own_step(t, carry):
        for c in range(cuts):
            for n, value in enumerate(result(before + t, c)):
                dkv_ref[place(t, turn, blocks), n, c * tile:(c + 1) * tile] = value
        return carry

    lax.fori_loop(0, before, halo_step, 0)
    lax.fori_loop(0, blocks, own_step, 0, unroll=2)

    def wait_step(i, carry):
        y_copy(i).wait()
        return carry

    lax.fori_loop(0, blocks, wait_step, 0)


def attention(meta, ends, k, kt, x, before):
    blocks, _, rows, dim = x.shape
    group = x.shape[1] // 2
    tiles, _, tile, _ = k.shape
    cuts = rows // tile
    hbm = pl.BlockSpec(memory_space=pl.ANY)
    most = before * cuts + 1
    return pl.pallas_call(
        functools.partial(attention_kernel, blocks=blocks, before=before, group=group),
        out_shape=(
            jax.ShapeDtypeStruct(x.shape, jnp.bfloat16),
            jax.ShapeDtypeStruct((blocks, 2, rows, dim), jnp.float32),
            jax.ShapeDtypeStruct((before, 2, rows, dim), jnp.bfloat16),
        ),
        in_specs=[SMEM, VMEM, hbm, hbm, VMEM],
        out_specs=(hbm, VMEM, VMEM),
        scratch_shapes=[
            pltpu.VMEM(k.shape, k.dtype),
            pltpu.VMEM(kt.shape, kt.dtype),
            pltpu.VMEM((tiles, 2, tile, dim), jnp.float32),
            pltpu.VMEM((most * tile, group * tile), jnp.float32),
            pltpu.VMEM((most * tile, group * tile), jnp.float32),
            pltpu.VMEM(x.shape, jnp.bfloat16),
            pltpu.SemaphoreType.DMA,
            pltpu.SemaphoreType.DMA,
            pltpu.SemaphoreType.DMA((blocks,)),
        ],
        compiler_params=pltpu.CompilerParams(vmem_limit_bytes=60 * 1024 * 1024),
        cost_estimate=pl.CostEstimate(flops=5 * 10**9, bytes_accessed=12 * 2**20, transcendentals=4 * 10**6),
    )(meta, ends, k, kt, x)


def after(array, other):
    return lax.optimization_barrier((array, other))[0]


def body(queries, keys, values, out_grad, doc_lengths):
    rows, heads, dim = queries.shape
    kv_heads = keys.shape[1]
    group = heads // kv_heads
    blocks = kv_heads
    parts = lax.axis_size("ctx") // blocks
    before = WINDOW // rows
    tile = TILE
    turns = [(p % 2) * (blocks // 2) for p in range(parts)]
    groups = [[p * blocks + (r + turns[p]) % blocks for r in range(blocks)] for p in range(parts)]
    onward = [(groups[p][r], groups[p + 1][r]) for p in range(parts - 1) for r in range(blocks)]
    part = lax.axis_index("ctx") // blocks

    docs = doc_lengths.shape[0]
    upto = jnp.arange(docs)[:, None] >= jnp.arange(docs)[None, :]
    ends = jnp.sum(jnp.where(upto, doc_lengths[None, :], 0), axis=1)
    base = part * blocks * rows
    turn = lax.rem(part, 2) * (blocks // 2)
    position = base + jnp.arange(blocks * (rows // tile), dtype=jnp.int32) * tile
    start = jnp.max(jnp.where(ends[None, :] <= position[:, None], ends[None, :], 0), axis=1)
    first = jnp.maximum(jnp.maximum(start, position - (WINDOW - 1)), 0)
    meta = jnp.concatenate((position // tile - first // tile + 1, jnp.stack((base, turn)))).astype(jnp.int32)
    ends = ends[:, None].astype(jnp.int32)

    def exchange(array):
        return lax.all_to_all(array, "ctx", 0, 0, axis_index_groups=groups)

    def by_head(array):
        array = jnp.swapaxes(array, 0, 1)
        return array.reshape(kv_heads, array.shape[0] // kv_heads, array.shape[1], dim)

    def by_token(array):
        array = array.reshape(array.shape[0] * array.shape[1], array.shape[2], dim)
        return jnp.swapaxes(array, 0, 1)

    kv = exchange(jnp.concatenate((by_head(keys), by_head(values)), 1))
    tail = jnp.stack([kv[(blocks - before + t + turns[0]) % blocks] for t in range(before)]) if turns[0] else kv[blocks - before:]
    halo = lax.ppermute(tail, "ctx", onward)
    packed = jnp.concatenate([by_head(a) for a in (queries, out_grad)], 1)
    x = exchange(after(packed, kv))
    k, kt = prepare(jnp.stack((base, turn)).astype(jnp.int32), kv, halo, tile)
    y, dkv, dhalo = attention(meta, ends, k, kt, x, before)
    dhalo = lax.ppermute(dhalo, "ctx", [(b, a) for a, b in onward])
    y = exchange(y)
    still = blocks - before
    dkv = jnp.concatenate((dkv[:still], dkv[still:] + dhalo.astype(jnp.float32)), 0).astype(jnp.bfloat16)
    dkv = exchange(after(dkv, y))
    dk, dv = (jnp.swapaxes(dkv[:, n], 0, 1) for n in range(2))
    return by_token(y[:, :group]), by_token(y[:, group:]), dk, dv


def solution(mesh):
    spec = P(("dp", "ctx"), "head", None)
    return jax.shard_map(
        body,
        mesh=mesh,
        in_specs=(spec, spec, spec, spec, P("dp")),
        out_specs=(spec, spec, spec, spec),
        check_vma=False,
    )
```

```python
import functools

import jax
import jax.numpy as jnp
from jax import lax
from jax.experimental import pallas as pl
from jax.experimental.pallas import tpu as pltpu
from jax.sharding import PartitionSpec as P

WINDOW = 1024
SCALING = 168.0 ** (-0.5)
LOG2E = 1.4426950408889634
NEG = -1e30
TILE = 128
VMEM_LIMIT = 48 * 1024 * 1024
HBM = pl.ANY
JOINT = (2, 6)

NT = (((1,), (1,)), ((), ()))
NN = (((1,), (0,)), ((), ()))

VMEM = pl.BlockSpec(memory_space=pltpu.VMEM)
SMEM = pl.BlockSpec(memory_space=pltpu.SMEM)


def dot(a, b, dims):
    return lax.dot_general(a, b, dims, preferred_element_type=jnp.float32)


def place(i, turn, blocks):
    return lax.rem(i + turn, blocks)


def prepare_kernel(meta_ref, kv_ref, halo_ref, k_hbm, kt_hbm, k_ref, kt_ref, k_sem, kt_sem, *, blocks, tile):
    before = halo_ref.shape[0]
    cuts = kv_ref.shape[2] // tile
    turn = meta_ref[1]

    def put(source, index, at):
        for n in range(2):
            for c in range(cuts):
                part = source[index, n, c * tile:(c + 1) * tile]
                k_ref[at * cuts + c, n] = part
                kt_ref[at * cuts + c, n] = part.T

    def halo_step(t, carry):
        put(halo_ref, t, t)
        return carry

    def own_step(t, carry):
        put(kv_ref, place(t, turn, blocks), before + t)
        return carry

    lax.fori_loop(0, before, halo_step, 0)
    lax.fori_loop(0, blocks, own_step, 0, unroll=2)
    copies = [pltpu.make_async_copy(k_ref, k_hbm, k_sem), pltpu.make_async_copy(kt_ref, kt_hbm, kt_sem)]
    for copy in copies:
        copy.start()
    for copy in copies:
        copy.wait()


def prepare(meta, kv, halo, tile):
    blocks, _, rows, dim = kv.shape
    tiles = (halo.shape[0] + blocks) * (rows // tile)
    outs = (
        jax.ShapeDtypeStruct((tiles, 2, tile, dim), kv.dtype),
        jax.ShapeDtypeStruct((tiles, 2, dim, tile), kv.dtype),
    )
    hbm = pl.BlockSpec(memory_space=HBM)
    return pl.pallas_call(
        functools.partial(prepare_kernel, blocks=blocks, tile=tile),
        out_shape=outs,
        in_specs=[SMEM, VMEM, VMEM],
        out_specs=(hbm, hbm),
        scratch_shapes=[pltpu.VMEM(o.shape, o.dtype) for o in outs] + [pltpu.SemaphoreType.DMA] * 2,
        compiler_params=pltpu.CompilerParams(vmem_limit_bytes=12 * 1024 * 1024),
        cost_estimate=pl.CostEstimate(flops=10**6, bytes_accessed=6 * 2**20, transcendentals=0),
    )(meta, kv, halo)


def attention_kernel(
    meta_ref, ends_ref, k_hbm, kt_hbm, x_hbm, y_hbm, acc_hbm,
    k_ref, kt_ref, x_ref, acc_ref, s_ref, g_ref, y_ref, k_sem, kt_sem, x_sem, y_sem, acc_sem, *, blocks, before, group,
):
    rows, dim = x_ref.shape[2:]
    tile = k_ref.shape[2]
    wide = group * tile
    cuts = rows // tile
    halo = before * cuts
    base, turn = meta_ref[blocks * cuts], meta_ref[blocks * cuts + 1]

    def tile_copies(block):
        near = pl.ds(halo + block * cuts, cuts)
        return [pltpu.make_async_copy(h.at[near], r.at[near], sem.at[block]) for h, r, sem in sources]

    sources = ((k_hbm, k_ref, k_sem), (kt_hbm, kt_ref, kt_sem))
    start_copies = [
        pltpu.make_async_copy(h.at[pl.ds(0, halo + cuts)], r.at[pl.ds(0, halo + cuts)], sem.at[0]) for h, r, sem in sources
    ]

    def x_copy(at):
        return pltpu.make_async_copy(x_hbm.at[at], x_ref.at[at], x_sem.at[at])

    x_copy(place(0, turn, blocks)).start()
    for copy in start_copies:
        copy.start()

    def fetch_step(block, carry):
        x_copy(place(block, turn, blocks)).start()
        for copy in tile_copies(block):
            copy.start()
        return carry

    lax.fori_loop(1, blocks, fetch_step, 0)

    def zero_step(t, carry):
        acc_ref[t] = jnp.zeros(acc_ref.shape[1:], jnp.float32)
        return carry

    lax.fori_loop(0, before, zero_step, 0)

    def acc_at(t, m):
        return t // cuts, m, pl.ds(pl.multiple_of(lax.rem(t, cuts) * tile, tile), tile)

    lane = lax.rem(lax.broadcasted_iota(jnp.int32, (1, wide), 1), tile)
    diff = lane - lax.broadcasted_iota(jnp.int32, (2 * tile, wide), 0)

    def y_copy(at):
        return pltpu.make_async_copy(y_ref.at[at], y_hbm.at[at], y_sem.at[at])

    def acc_copy(t):
        return pltpu.make_async_copy(acc_ref.at[t], acc_hbm.at[t], acc_sem.at[t])

    def scores(slot, i, at, piece, count):
        first = halo + i - (count - 1)
        span = pl.ds(piece * tile, tile)
        q = x_ref[at, 0:group, span].reshape(wide, dim)
        do = x_ref[at, group:2 * group, span].reshape(wide, dim)
        pos = base + i * tile + lane
        ends = ends_ref[...]
        start = jnp.max(jnp.where(ends <= pos, ends, 0), axis=0, keepdims=True)
        reach = pos - jnp.maximum(start, pos - (WINDOW - 1))
        chunks = [(0, 1)] * (count % 2) + [(a, 2) for a in range(count % 2, count, 2)]
        top = None
        for a, n in chunks:
            raw = dot(k_ref[pl.ds(first + a, n), 0].reshape(n * tile, dim), q, NT)
            offset = (count - 1 - a) * tile
            keep = diff[:n * tile] <= reach - offset
            if a + n == count:
                keep = keep & (diff[:n * tile] >= -offset)
            raw = jnp.where(keep, raw, NEG)
            s_ref[slot, a * tile:(a + n) * tile] = raw
            here = jnp.max(raw, axis=0, keepdims=True)
            top = here if top is None else jnp.maximum(top, here)
            g_ref[slot, a * tile:(a + n) * tile] = dot(
                k_ref[pl.ds(first + a, n), 1].reshape(n * tile, dim), do, NT
            )
        return first, q, do, chunks, top

    def weigh(slot, state):
        first, q, do, chunks, top = state
        total = mixed = 0.0
        for a, n in chunks:
            p = jnp.exp2((s_ref[slot, a * tile:(a + n) * tile] - top) * (SCALING * LOG2E))
            s_ref[slot, a * tile:(a + n) * tile] = p
            total += jnp.sum(p, axis=0, keepdims=True)
            mixed += jnp.sum(p * g_ref[slot, a * tile:(a + n) * tile], axis=0, keepdims=True)
        inverse = 1.0 / total
        return first, q, do, chunks, inverse, mixed * inverse

    def gradients(slot, at, piece, count, state):
        first, q, do, chunks, inverse, row_total = state
        span = pl.ds(piece * tile, tile)
        out = dq = 0.0
        for a, n in chunks:
            w = s_ref[slot, a * tile:(a + n) * tile] * inverse
            wb = w.astype(jnp.bfloat16)
            ds = (w * (g_ref[slot, a * tile:(a + n) * tile] - row_total)).astype(jnp.bfloat16)
            kt, vt = (
                jnp.concatenate([kt_ref[first + a + c, m] for c in range(n)], axis=1) for m in range(2)
            )
            out += dot(vt, wb, NN)
            dq += dot(kt, ds, NN)
            for m, part in enumerate((dot(ds, q, NN), dot(wb, do, NN))):
                for c in range(n):
                    here = acc_at(first + a + c, m)
                    if a + c == count - 1:
                        acc_ref[here] = part[c * tile:]
                    else:
                        acc_ref[here] += part[c * tile:(c + 1) * tile]
        y_ref[at, 0:group, span] = out.T.astype(jnp.bfloat16).reshape(group, tile, dim)
        y_ref[at, group:2 * group, span] = (SCALING * dq).T.astype(jnp.bfloat16).reshape(group, tile, dim)

    def query_tiles(block, at, pieces, count):
        states = [scores(slot, block * cuts + c, at, c, count) for slot, c in enumerate(pieces)]
        states = [weigh(slot, state) for slot, state in enumerate(states)]
        for slot, c in enumerate(pieces):
            gradients(slot, at, c, count, states[slot])

    def block_step(block, carry):
        at = place(block, turn, blocks)
        counts = [meta_ref[block * cuts + c] for c in range(cuts)]
        most = functools.reduce(jnp.maximum, counts)
        x_copy(at).wait()

        @pl.when(block == 0)
        def _():
            for copy in start_copies:
                copy.wait()

        @pl.when(block > 0)
        def _():
            for copy in tile_copies(block):
                copy.wait()

        for n in range(JOINT[0], JOINT[1]):
            here = (most == n) if n > JOINT[0] else (most <= n)
            pl.when(here)(functools.partial(query_tiles, block, at, list(range(cuts)), n))
        for c in range(cuts):
            for n in range(1, halo + 2):
                here = (counts[c] == n) & (most >= JOINT[1])
                pl.when(here)(functools.partial(query_tiles, block, at, [c], n))
        y_copy(at).start()
        acc_copy(block).start()
        return carry

    lax.fori_loop(0, blocks, block_step, 0)
    for t in range(blocks, blocks + before):
        acc_copy(t).start()

    def wait_step(i, carry):
        y_copy(i).wait()
        return carry

    def acc_wait_step(t, carry):
        acc_copy(t).wait()
        return carry

    lax.fori_loop(0, blocks, wait_step, 0)
    lax.fori_loop(0, blocks + before, acc_wait_step, 0)


def attention(meta, ends, k, kt, x, before):
    blocks, _, rows, dim = x.shape
    group = x.shape[1] // 2
    tiles, _, tile, _ = k.shape
    cuts = rows // tile
    hbm = pl.BlockSpec(memory_space=HBM)
    any_space = pl.BlockSpec(memory_space=pl.ANY)
    most = before * cuts + 1
    return pl.pallas_call(
        functools.partial(attention_kernel, blocks=blocks, before=before, group=group),
        out_shape=(
            jax.ShapeDtypeStruct(x.shape, jnp.bfloat16),
            jax.ShapeDtypeStruct((before + blocks, 2, rows, dim), jnp.float32),
        ),
        in_specs=[SMEM, VMEM, any_space, any_space, any_space],
        out_specs=(any_space, any_space),
        scratch_shapes=[
            pltpu.VMEM(k.shape, k.dtype),
            pltpu.VMEM(kt.shape, kt.dtype),
            pltpu.VMEM(x.shape, x.dtype),
            pltpu.VMEM((before + blocks, 2, rows, dim), jnp.float32),
            pltpu.VMEM((cuts, most * tile, group * tile), jnp.float32),
            pltpu.VMEM((cuts, most * tile, group * tile), jnp.float32),
            pltpu.VMEM(x.shape, jnp.bfloat16),
            pltpu.SemaphoreType.DMA((blocks,)),
            pltpu.SemaphoreType.DMA((blocks,)),
            pltpu.SemaphoreType.DMA((blocks,)),
            pltpu.SemaphoreType.DMA((blocks,)),
            pltpu.SemaphoreType.DMA((before + blocks,)),
        ],
        compiler_params=pltpu.CompilerParams(vmem_limit_bytes=VMEM_LIMIT),
        cost_estimate=pl.CostEstimate(flops=5 * 10**9, bytes_accessed=12 * 2**20, transcendentals=4 * 10**6),
    )(meta, ends, k, kt, x)


def after(array, other):
    return lax.optimization_barrier((array, other))[0]


def body(queries, keys, values, out_grad, doc_lengths):
    rows, heads, dim = queries.shape
    kv_heads = keys.shape[1]
    group = heads // kv_heads
    blocks = kv_heads
    parts = lax.axis_size("ctx") // blocks
    before = WINDOW // rows
    tile = TILE
    turns = [(p % 2) * (blocks // 2) for p in range(parts)]
    groups = [[p * blocks + (r + turns[p]) % blocks for r in range(blocks)] for p in range(parts)]
    onward = [(groups[p][r], groups[p + 1][r]) for p in range(parts - 1) for r in range(blocks)]
    part = lax.axis_index("ctx") // blocks

    docs = doc_lengths.shape[0]
    upto = jnp.arange(docs)[:, None] >= jnp.arange(docs)[None, :]
    ends = jnp.sum(jnp.where(upto, doc_lengths[None, :], 0), axis=1)
    base = part * blocks * rows
    turn = lax.rem(part, 2) * (blocks // 2)
    position = base + jnp.arange(blocks * (rows // tile), dtype=jnp.int32) * tile
    start = jnp.max(jnp.where(ends[None, :] <= position[:, None], ends[None, :], 0), axis=1)
    first = jnp.maximum(jnp.maximum(start, position - (WINDOW - 1)), 0)
    meta = jnp.concatenate((position // tile - first // tile + 1, jnp.stack((base, turn)))).astype(jnp.int32)
    ends = ends[:, None].astype(jnp.int32)

    def exchange(array):
        return lax.all_to_all(array, "ctx", 0, 0, axis_index_groups=groups)

    def by_head(array):
        array = jnp.swapaxes(array, 0, 1)
        return array.reshape(kv_heads, array.shape[0] // kv_heads, array.shape[1], dim)

    def by_token(array):
        array = array.reshape(array.shape[0] * array.shape[1], array.shape[2], dim)
        return jnp.swapaxes(array, 0, 1)

    kv = exchange(jnp.concatenate((by_head(keys), by_head(values)), 1))
    tail = jnp.stack([kv[(blocks - before + t + turns[0]) % blocks] for t in range(before)]) if turns[0] else kv[blocks - before:]
    halo = lax.ppermute(tail, "ctx", onward)
    packed = jnp.concatenate([by_head(a) for a in (queries, out_grad)], 1)
    x = exchange(after(packed, kv))
    k, kt = prepare(jnp.stack((base, turn)).astype(jnp.int32), kv, halo, tile)
    y, acc = attention(meta, ends, k, kt, x, before)
    acc = acc * jnp.where(jnp.arange(2) == 0, SCALING, 1.0).astype(jnp.float32)[:, None, None]
    dhalo = lax.ppermute(acc[:before].astype(jnp.bfloat16), "ctx", [(b, a) for a, b in onward])
    y = exchange(y)
    half = blocks // 2
    dkv = jnp.concatenate((acc[before:blocks], acc[blocks:] + dhalo.astype(jnp.float32)), 0)
    dkv = jnp.where(turn == 0, dkv, jnp.concatenate((dkv[half:], dkv[:half]), 0)).astype(jnp.bfloat16)
    dkv = exchange(after(dkv, y))
    dk, dv = (jnp.swapaxes(dkv[:, n], 0, 1) for n in range(2))
    return by_token(y[:, :group]), by_token(y[:, group:]), dk, dv


def solution(mesh):
    spec = P(("dp", "ctx"), "head", None)
    return jax.shard_map(
        body,
        mesh=mesh,
        in_specs=(spec, spec, spec, spec, P("dp")),
        out_specs=(spec, spec, spec, spec),
        check_vma=False,
    )
```

```python
import functools

import jax
import jax.numpy as jnp
from jax import lax
from jax.experimental import pallas as pl
from jax.experimental.pallas import tpu as pltpu
from jax.sharding import PartitionSpec as P

WINDOW = 1024
SCALING = 168.0 ** (-0.5)
LOG2E = 1.4426950408889634
NEG = -1e30
TILE = 128
VMEM_LIMIT = 48 * 1024 * 1024
HBM = pl.ANY
JOINT = (2, 6)

NT = (((1,), (1,)), ((), ()))
NN = (((1,), (0,)), ((), ()))

VMEM = pl.BlockSpec(memory_space=pltpu.VMEM)
SMEM = pl.BlockSpec(memory_space=pltpu.SMEM)


def dot(a, b, dims):
    return lax.dot_general(a, b, dims, preferred_element_type=jnp.float32)


def place(i, turn, blocks):
    return lax.rem(i + turn, blocks)


def prepare_kernel(meta_ref, kv_ref, halo_ref, k_hbm, kt_hbm, k_ref, kt_ref, k_sem, kt_sem, *, blocks, tile):
    before = halo_ref.shape[0]
    cuts = kv_ref.shape[2] // tile
    turn = meta_ref[1]

    def put(source, index, at):
        for n in range(2):
            for c in range(cuts):
                part = source[index, n, c * tile:(c + 1) * tile]
                k_ref[at * cuts + c, n] = part
                kt_ref[at * cuts + c, n] = part.T

    def halo_step(t, carry):
        put(halo_ref, t, t)
        return carry

    def own_step(t, carry):
        put(kv_ref, place(t, turn, blocks), before + t)
        return carry

    lax.fori_loop(0, before, halo_step, 0)
    lax.fori_loop(0, blocks, own_step, 0, unroll=2)
    copies = [pltpu.make_async_copy(k_ref, k_hbm, k_sem), pltpu.make_async_copy(kt_ref, kt_hbm, kt_sem)]
    for copy in copies:
        copy.start()
    for copy in copies:
        copy.wait()


def prepare(meta, kv, halo, tile):
    blocks, _, rows, dim = kv.shape
    tiles = (halo.shape[0] + blocks) * (rows // tile)
    outs = (
        jax.ShapeDtypeStruct((tiles, 2, tile, dim), kv.dtype),
        jax.ShapeDtypeStruct((tiles, 2, dim, tile), kv.dtype),
    )
    hbm = pl.BlockSpec(memory_space=HBM)
    return pl.pallas_call(
        functools.partial(prepare_kernel, blocks=blocks, tile=tile),
        out_shape=outs,
        in_specs=[SMEM, VMEM, VMEM],
        out_specs=(hbm, hbm),
        scratch_shapes=[pltpu.VMEM(o.shape, o.dtype) for o in outs] + [pltpu.SemaphoreType.DMA] * 2,
        compiler_params=pltpu.CompilerParams(vmem_limit_bytes=12 * 1024 * 1024),
        cost_estimate=pl.CostEstimate(flops=10**6, bytes_accessed=6 * 2**20, transcendentals=0),
    )(meta, kv, halo)


def attention_kernel(
    meta_ref, ends_ref, k_hbm, kt_hbm, x_hbm, y_hbm, acc_hbm, dhalo_hbm,
    k_ref, kt_ref, x_ref, acc_ref, s_ref, g_ref, y_ref, dhalo_ref, k_sem, kt_sem, x_sem, y_sem, acc_sem, dhalo_sem, *, blocks, before, group,
):
    rows, dim = x_ref.shape[2:]
    tile = k_ref.shape[2]
    wide = group * tile
    cuts = rows // tile
    halo = before * cuts
    base, turn = meta_ref[blocks * cuts], meta_ref[blocks * cuts + 1]

    def tile_copies(block):
        near = pl.ds(halo + block * cuts, cuts)
        return [pltpu.make_async_copy(h.at[near], r.at[near], sem.at[block]) for h, r, sem in sources]

    sources = ((k_hbm, k_ref, k_sem), (kt_hbm, kt_ref, kt_sem))
    start_copies = [
        pltpu.make_async_copy(h.at[pl.ds(0, halo + cuts)], r.at[pl.ds(0, halo + cuts)], sem.at[0]) for h, r, sem in sources
    ]

    def x_copy(at):
        return pltpu.make_async_copy(x_hbm.at[at], x_ref.at[at], x_sem.at[at])

    x_copy(place(0, turn, blocks)).start()
    for copy in start_copies:
        copy.start()

    def fetch_step(block, carry):
        x_copy(place(block, turn, blocks)).start()
        for copy in tile_copies(block):
            copy.start()
        return carry

    lax.fori_loop(1, blocks, fetch_step, 0)

    def zero_step(t, carry):
        acc_ref[t] = jnp.zeros(acc_ref.shape[1:], jnp.float32)
        return carry

    lax.fori_loop(0, before, zero_step, 0)

    def acc_at(t, m):
        return t // cuts, m, pl.ds(pl.multiple_of(lax.rem(t, cuts) * tile, tile), tile)

    lane = lax.rem(lax.broadcasted_iota(jnp.int32, (1, wide), 1), tile)
    diff = lane - lax.broadcasted_iota(jnp.int32, (2 * tile, wide), 0)

    def y_copy(at):
        return pltpu.make_async_copy(y_ref.at[at], y_hbm.at[at], y_sem.at[at])

    def acc_copy(t):
        return pltpu.make_async_copy(acc_ref.at[before + t], acc_hbm.at[place(t, turn, blocks)], acc_sem.at[t])

    def dhalo_copy(t):
        return pltpu.make_async_copy(dhalo_ref.at[t], dhalo_hbm.at[t], dhalo_sem.at[t])

    def scores(slot, i, at, piece, count):
        first = halo + i - (count - 1)
        span = pl.ds(piece * tile, tile)
        q = x_ref[at, 0:group, span].reshape(wide, dim)
        do = x_ref[at, group:2 * group, span].reshape(wide, dim)
        pos = base + i * tile + lane
        ends = ends_ref[...]
        start = jnp.max(jnp.where(ends <= pos, ends, 0), axis=0, keepdims=True)
        reach = pos - jnp.maximum(start, pos - (WINDOW - 1))
        chunks = [(0, 1)] * (count % 2) + [(a, 2) for a in range(count % 2, count, 2)]
        top = None
        for a, n in chunks:
            raw = dot(k_ref[pl.ds(first + a, n), 0].reshape(n * tile, dim), q, NT)
            offset = (count - 1 - a) * tile
            keep = diff[:n * tile] <= reach - offset
            if a + n == count:
                keep = keep & (diff[:n * tile] >= -offset)
            raw = jnp.where(keep, raw, NEG)
            s_ref[slot, a * tile:(a + n) * tile] = raw
            here = jnp.max(raw, axis=0, keepdims=True)
            top = here if top is None else jnp.maximum(top, here)
            g_ref[slot, a * tile:(a + n) * tile] = dot(
                k_ref[pl.ds(first + a, n), 1].reshape(n * tile, dim), do, NT
            )
        return first, q, do, chunks, top

    def weigh(slot, state):
        first, q, do, chunks, top = state
        total = mixed = 0.0
        for a, n in chunks:
            p = jnp.exp2((s_ref[slot, a * tile:(a + n) * tile] - top) * (SCALING * LOG2E))
            s_ref[slot, a * tile:(a + n) * tile] = p
            total += jnp.sum(p, axis=0, keepdims=True)
            mixed += jnp.sum(p * g_ref[slot, a * tile:(a + n) * tile], axis=0, keepdims=True)
        inverse = 1.0 / total
        return first, q, do, chunks, inverse, mixed * inverse

    def gradients(slot, at, piece, count, state):
        first, q, do, chunks, inverse, row_total = state
        span = pl.ds(piece * tile, tile)
        out = dq = 0.0
        for a, n in chunks:
            w = s_ref[slot, a * tile:(a + n) * tile] * inverse
            wb = w.astype(jnp.bfloat16)
            ds = (w * (g_ref[slot, a * tile:(a + n) * tile] - row_total)).astype(jnp.bfloat16)
            kt, vt = (
                jnp.concatenate([kt_ref[first + a + c, m] for c in range(n)], axis=1) for m in range(2)
            )
            out += dot(vt, wb, NN)
            dq += dot(kt, ds, NN)
            for m, part in enumerate((dot(ds, q, NN), dot(wb, do, NN))):
                for c in range(n):
                    here = acc_at(first + a + c, m)
                    if a + c == count - 1:
                        acc_ref[here] = part[c * tile:]
                    else:
                        acc_ref[here] += part[c * tile:(c + 1) * tile]
        y_ref[at, 0:group, span] = out.T.astype(jnp.bfloat16).reshape(group, tile, dim)
        y_ref[at, group:2 * group, span] = (SCALING * dq).T.astype(jnp.bfloat16).reshape(group, tile, dim)

    def query_tiles(block, at, pieces, count):
        states = [scores(slot, block * cuts + c, at, c, count) for slot, c in enumerate(pieces)]
        states = [weigh(slot, state) for slot, state in enumerate(states)]
        for slot, c in enumerate(pieces):
            gradients(slot, at, c, count, states[slot])

    def block_step(block, carry):
        at = place(block, turn, blocks)
        counts = [meta_ref[block * cuts + c] for c in range(cuts)]
        most = functools.reduce(jnp.maximum, counts)
        x_copy(at).wait()

        @pl.when(block == 0)
        def _():
            for copy in start_copies:
                copy.wait()

        @pl.when(block > 0)
        def _():
            for copy in tile_copies(block):
                copy.wait()

        for n in range(JOINT[0], JOINT[1]):
            here = (most == n) if n > JOINT[0] else (most <= n)
            pl.when(here)(functools.partial(query_tiles, block, at, list(range(cuts)), n))
        for c in range(cuts):
            for n in range(1, halo + 2):
                here = (counts[c] == n) & (most >= JOINT[1])
                pl.when(here)(functools.partial(query_tiles, block, at, [c], n))
        y_copy(at).start()

        @pl.when(block < before)
        def _():
            dhalo_ref[block, 0] = (SCALING * acc_ref[block, 0]).astype(jnp.bfloat16)
            dhalo_ref[block, 1] = acc_ref[block, 1].astype(jnp.bfloat16)
            dhalo_copy(block).start()

        @pl.when(block >= before)
        def _():
            acc_copy(block - before).start()

        return carry

    lax.fori_loop(0, blocks, block_step, 0)
    for t in range(blocks - before, blocks):
        acc_copy(t).start()

    def wait_step(i, carry):
        y_copy(i).wait()
        acc_copy(i).wait()
        return carry

    def halo_wait_step(t, carry):
        dhalo_copy(t).wait()
        return carry

    lax.fori_loop(0, blocks, wait_step, 0)
    lax.fori_loop(0, before, halo_wait_step, 0)


def attention(meta, ends, k, kt, x, before):
    blocks, _, rows, dim = x.shape
    group = x.shape[1] // 2
    tiles, _, tile, _ = k.shape
    cuts = rows // tile
    hbm = pl.BlockSpec(memory_space=HBM)
    any_space = pl.BlockSpec(memory_space=pl.ANY)
    most = before * cuts + 1
    return pl.pallas_call(
        functools.partial(attention_kernel, blocks=blocks, before=before, group=group),
        out_shape=(
            jax.ShapeDtypeStruct(x.shape, jnp.bfloat16),
            jax.ShapeDtypeStruct((blocks, 2, rows, dim), jnp.float32),
            jax.ShapeDtypeStruct((before, 2, rows, dim), jnp.bfloat16),
        ),
        in_specs=[SMEM, VMEM, any_space, any_space, any_space],
        out_specs=(any_space, any_space, any_space),
        scratch_shapes=[
            pltpu.VMEM(k.shape, k.dtype),
            pltpu.VMEM(kt.shape, kt.dtype),
            pltpu.VMEM(x.shape, x.dtype),
            pltpu.VMEM((before + blocks, 2, rows, dim), jnp.float32),
            pltpu.VMEM((cuts, most * tile, group * tile), jnp.float32),
            pltpu.VMEM((cuts, most * tile, group * tile), jnp.float32),
            pltpu.VMEM(x.shape, jnp.bfloat16),
            pltpu.VMEM((before, 2, rows, dim), jnp.bfloat16),
            pltpu.SemaphoreType.DMA((blocks,)),
            pltpu.SemaphoreType.DMA((blocks,)),
            pltpu.SemaphoreType.DMA((blocks,)),
            pltpu.SemaphoreType.DMA((blocks,)),
            pltpu.SemaphoreType.DMA((blocks,)),
            pltpu.SemaphoreType.DMA((before,)),
        ],
        compiler_params=pltpu.CompilerParams(vmem_limit_bytes=VMEM_LIMIT),
        cost_estimate=pl.CostEstimate(flops=5 * 10**9, bytes_accessed=12 * 2**20, transcendentals=4 * 10**6),
    )(meta, ends, k, kt, x)


def after(array, other):
    return lax.optimization_barrier((array, other))[0]


def body(queries, keys, values, out_grad, doc_lengths):
    rows, heads, dim = queries.shape
    kv_heads = keys.shape[1]
    group = heads // kv_heads
    blocks = kv_heads
    parts = lax.axis_size("ctx") // blocks
    before = WINDOW // rows
    tile = TILE
    turns = [(p % 2) * (blocks // 2) for p in range(parts)]
    groups = [[p * blocks + (r + turns[p]) % blocks for r in range(blocks)] for p in range(parts)]
    onward = [(groups[p][r], groups[p + 1][r]) for p in range(parts - 1) for r in range(blocks)]
    part = lax.axis_index("ctx") // blocks

    docs = doc_lengths.shape[0]
    upto = jnp.arange(docs)[:, None] >= jnp.arange(docs)[None, :]
    ends = jnp.sum(jnp.where(upto, doc_lengths[None, :], 0), axis=1)
    base = part * blocks * rows
    turn = lax.rem(part, 2) * (blocks // 2)
    position = base + jnp.arange(blocks * (rows // tile), dtype=jnp.int32) * tile
    start = jnp.max(jnp.where(ends[None, :] <= position[:, None], ends[None, :], 0), axis=1)
    first = jnp.maximum(jnp.maximum(start, position - (WINDOW - 1)), 0)
    meta = jnp.concatenate((position // tile - first // tile + 1, jnp.stack((base, turn)))).astype(jnp.int32)
    ends = ends[:, None].astype(jnp.int32)

    def exchange(array):
        return lax.all_to_all(array, "ctx", 0, 0, axis_index_groups=groups)

    def by_head(array):
        array = jnp.swapaxes(array, 0, 1)
        return array.reshape(kv_heads, array.shape[0] // kv_heads, array.shape[1], dim)

    def by_token(array):
        array = array.reshape(array.shape[0] * array.shape[1], array.shape[2], dim)
        return jnp.swapaxes(array, 0, 1)

    kv = exchange(jnp.concatenate((by_head(keys), by_head(values)), 1))
    tail = jnp.stack([kv[(blocks - before + t + turns[0]) % blocks] for t in range(before)]) if turns[0] else kv[blocks - before:]
    halo = lax.ppermute(tail, "ctx", onward)
    packed = jnp.concatenate([by_head(a) for a in (queries, out_grad)], 1)
    x = exchange(after(packed, kv))
    k, kt = prepare(jnp.stack((base, turn)).astype(jnp.int32), kv, halo, tile)
    y, dkv, dhalo = attention(meta, ends, k, kt, x, before)
    dhalo = lax.ppermute(dhalo, "ctx", [(b, a) for a, b in onward])
    y = exchange(y)
    factor = jnp.where(jnp.arange(2) == 0, SCALING, 1.0).astype(jnp.float32)[:, None, None]
    dhalo = jnp.pad(dhalo.astype(jnp.float32), ((blocks - before, 0), (0, 0), (0, 0), (0, 0)))
    dkv = (dkv * factor + dhalo).astype(jnp.bfloat16)
    dkv = exchange(after(dkv, y))
    dk, dv = (jnp.swapaxes(dkv[:, n], 0, 1) for n in range(2))
    return by_token(y[:, :group]), by_token(y[:, group:]), dk, dv


def solution(mesh):
    spec = P(("dp", "ctx"), "head", None)
    return jax.shard_map(
        body,
        mesh=mesh,
        in_specs=(spec, spec, spec, spec, P("dp")),
        out_specs=(spec, spec, spec, spec),
        check_vma=False,
    )
```

```python
import functools

import jax
import jax.numpy as jnp
from jax import lax
from jax.experimental import pallas as pl
from jax.experimental.pallas import tpu as pltpu
from jax.sharding import PartitionSpec as P

WINDOW = 1024
SCALING = 168.0 ** (-0.5)
LOG2E = 1.4426950408889634
NEG = -1e30
TILE = 128
VMEM_LIMIT = 48 * 1024 * 1024
HBM = pl.ANY
JOINT = (2, 6)

NT = (((1,), (1,)), ((), ()))
NN = (((1,), (0,)), ((), ()))

VMEM = pl.BlockSpec(memory_space=pltpu.VMEM)
SMEM = pl.BlockSpec(memory_space=pltpu.SMEM)


def dot(a, b, dims):
    return lax.dot_general(a, b, dims, preferred_element_type=jnp.float32)


def place(i, turn, blocks):
    return lax.rem(i + turn, blocks)


def prepare_kernel(meta_ref, kv_ref, halo_ref, k_hbm, kt_hbm, k_ref, kt_ref, k_sem, kt_sem, *, blocks, tile):
    before = halo_ref.shape[0]
    cuts = kv_ref.shape[2] // tile
    turn = meta_ref[1]

    def put(source, index, at):
        for n in range(2):
            for c in range(cuts):
                part = source[index, n, c * tile:(c + 1) * tile]
                k_ref[at * cuts + c, n] = part
                kt_ref[at * cuts + c, n] = part.T

    def halo_step(t, carry):
        put(halo_ref, t, t)
        return carry

    def own_step(t, carry):
        put(kv_ref, place(t, turn, blocks), before + t)
        return carry

    lax.fori_loop(0, before, halo_step, 0)
    lax.fori_loop(0, blocks, own_step, 0, unroll=2)
    copies = [pltpu.make_async_copy(k_ref, k_hbm, k_sem), pltpu.make_async_copy(kt_ref, kt_hbm, kt_sem)]
    for copy in copies:
        copy.start()
    for copy in copies:
        copy.wait()


def prepare(meta, kv, halo, tile):
    blocks, _, rows, dim = kv.shape
    tiles = (halo.shape[0] + blocks) * (rows // tile)
    outs = (
        jax.ShapeDtypeStruct((tiles, 2, tile, dim), kv.dtype),
        jax.ShapeDtypeStruct((tiles, 2, dim, tile), kv.dtype),
    )
    hbm = pl.BlockSpec(memory_space=HBM)
    return pl.pallas_call(
        functools.partial(prepare_kernel, blocks=blocks, tile=tile),
        out_shape=outs,
        in_specs=[SMEM, VMEM, VMEM],
        out_specs=(hbm, hbm),
        scratch_shapes=[pltpu.VMEM(o.shape, o.dtype) for o in outs] + [pltpu.SemaphoreType.DMA] * 2,
        compiler_params=pltpu.CompilerParams(vmem_limit_bytes=12 * 1024 * 1024),
        cost_estimate=pl.CostEstimate(flops=10**6, bytes_accessed=6 * 2**20, transcendentals=0),
    )(meta, kv, halo)


def attention_kernel(
    meta_ref, ends_ref, k_hbm, kt_hbm, x_hbm, y_hbm, acc_hbm, dhalo_hbm,
    k_ref, kt_ref, x_ref, acc_ref, s_ref, g_ref, y_ref, dhalo_ref, k_sem, kt_sem, x_sem, y_sem, acc_sem, dhalo_sem, *, blocks, before, group,
):
    rows, dim = x_ref.shape[2:]
    tile = k_ref.shape[2]
    wide = group * tile
    cuts = rows // tile
    halo = before * cuts
    base, turn = meta_ref[blocks * cuts], meta_ref[blocks * cuts + 1]

    def tile_copies(block):
        near = pl.ds(halo + block * cuts, cuts)
        return [pltpu.make_async_copy(h.at[near], r.at[near], sem.at[block]) for h, r, sem in sources]

    sources = ((k_hbm, k_ref, k_sem), (kt_hbm, kt_ref, kt_sem))
    start_copies = [
        pltpu.make_async_copy(h.at[pl.ds(0, halo + cuts)], r.at[pl.ds(0, halo + cuts)], sem.at[0]) for h, r, sem in sources
    ]

    def x_copy(at):
        return pltpu.make_async_copy(x_hbm.at[at], x_ref.at[at], x_sem.at[at])

    x_copy(place(0, turn, blocks)).start()
    for copy in start_copies:
        copy.start()

    def fetch_step(block, carry):
        x_copy(place(block, turn, blocks)).start()
        for copy in tile_copies(block):
            copy.start()
        return carry

    lax.fori_loop(1, blocks, fetch_step, 0)

    def zero_step(t, carry):
        acc_ref[t] = jnp.zeros(acc_ref.shape[1:], jnp.float32)
        return carry

    lax.fori_loop(0, before, zero_step, 0)

    def acc_at(t, m):
        return t // cuts, m, pl.ds(pl.multiple_of(lax.rem(t, cuts) * tile, tile), tile)

    lane = lax.rem(lax.broadcasted_iota(jnp.int32, (1, wide), 1), tile)
    diff = lane - lax.broadcasted_iota(jnp.int32, (2 * tile, wide), 0)

    def y_copy(at):
        return pltpu.make_async_copy(y_ref.at[at], y_hbm.at[at], y_sem.at[at])

    def acc_copy(t):
        return pltpu.make_async_copy(acc_ref.at[before + t], acc_hbm.at[place(t, turn, blocks)], acc_sem.at[t])

    def dhalo_copy(t):
        return pltpu.make_async_copy(dhalo_ref.at[t], dhalo_hbm.at[t], dhalo_sem.at[t])

    def scores(slot, i, at, piece, count):
        first = halo + i - (count - 1)
        span = pl.ds(piece * tile, tile)
        q = x_ref[at, 0:group, span].reshape(wide, dim)
        do = x_ref[at, group:2 * group, span].reshape(wide, dim)
        pos = base + i * tile + lane
        ends = ends_ref[...]
        start = jnp.max(jnp.where(ends <= pos, ends, 0), axis=0, keepdims=True)
        reach = pos - jnp.maximum(start, pos - (WINDOW - 1))
        chunks = [(0, 1)] * (count % 2) + [(a, 2) for a in range(count % 2, count, 2)]
        top = None
        for a, n in chunks:
            raw = dot(k_ref[pl.ds(first + a, n), 0].reshape(n * tile, dim), q, NT)
            offset = (count - 1 - a) * tile
            keep = diff[:n * tile] <= reach - offset
            if a + n == count:
                keep = keep & (diff[:n * tile] >= -offset)
            raw = jnp.where(keep, raw, NEG)
            s_ref[slot, a * tile:(a + n) * tile] = raw
            here = jnp.max(raw, axis=0, keepdims=True)
            top = here if top is None else jnp.maximum(top, here)
            g_ref[slot, a * tile:(a + n) * tile] = dot(
                k_ref[pl.ds(first + a, n), 1].reshape(n * tile, dim), do, NT
            )
        return first, q, do, chunks, top

    def weigh(slot, state):
        first, q, do, chunks, top = state
        total = mixed = 0.0
        for a, n in chunks:
            p = jnp.exp2((s_ref[slot, a * tile:(a + n) * tile] - top) * (SCALING * LOG2E))
            s_ref[slot, a * tile:(a + n) * tile] = p
            total += jnp.sum(p, axis=0, keepdims=True)
            mixed += jnp.sum(p * g_ref[slot, a * tile:(a + n) * tile], axis=0, keepdims=True)
        inverse = 1.0 / total
        return first, q, do, chunks, inverse, mixed * inverse

    def gradients(slot, at, piece, count, state):
        first, q, do, chunks, inverse, row_total = state
        span = pl.ds(piece * tile, tile)
        out = dq = 0.0
        for a, n in chunks:
            w = s_ref[slot, a * tile:(a + n) * tile] * inverse
            wb = w.astype(jnp.bfloat16)
            ds = (w * (g_ref[slot, a * tile:(a + n) * tile] - row_total)).astype(jnp.bfloat16)
            kt, vt = (
                jnp.concatenate([kt_ref[first + a + c, m] for c in range(n)], axis=1) for m in range(2)
            )
            out += dot(vt, wb, NN)
            dq += dot(kt, ds, NN)
            for m, part in enumerate((dot(ds, q, NN), dot(wb, do, NN))):
                for c in range(n):
                    here = acc_at(first + a + c, m)
                    if a + c == count - 1:
                        acc_ref[here] = part[c * tile:]
                    else:
                        acc_ref[here] += part[c * tile:(c + 1) * tile]
        y_ref[at, 0:group, span] = out.T.astype(jnp.bfloat16).reshape(group, tile, dim)
        y_ref[at, group:2 * group, span] = (SCALING * dq).T.astype(jnp.bfloat16).reshape(group, tile, dim)

    def query_tiles(block, at, pieces, count):
        states = [scores(slot, block * cuts + c, at, c, count) for slot, c in enumerate(pieces)]
        states = [weigh(slot, state) for slot, state in enumerate(states)]
        for slot, c in enumerate(pieces):
            gradients(slot, at, c, count, states[slot])

    def block_step(block, carry):
        at = place(block, turn, blocks)
        counts = [meta_ref[block * cuts + c] for c in range(cuts)]
        most = functools.reduce(jnp.maximum, counts)
        x_copy(at).wait()

        @pl.when(block == 0)
        def _():
            for copy in start_copies:
                copy.wait()

        @pl.when(block > 0)
        def _():
            for copy in tile_copies(block):
                copy.wait()

        for n in range(JOINT[0], JOINT[1]):
            here = (most == n) if n > JOINT[0] else (most <= n)
            pl.when(here)(functools.partial(query_tiles, block, at, list(range(cuts)), n))
        for c in range(cuts):
            for n in range(1, halo + 2):
                here = (counts[c] == n) & (most >= JOINT[1])
                pl.when(here)(functools.partial(query_tiles, block, at, [c], n))
        y_copy(at).start()

        @pl.when(block < before)
        def _():
            dhalo_ref[block, 0] = (SCALING * acc_ref[block, 0]).astype(jnp.bfloat16)
            dhalo_ref[block, 1] = acc_ref[block, 1].astype(jnp.bfloat16)
            dhalo_copy(block).start()

        @pl.when(block >= before)
        def _():
            acc_copy(block - before).start()

        return carry

    lax.fori_loop(0, blocks, block_step, 0)
    for t in range(blocks - before, blocks):
        acc_copy(t).start()

    def wait_step(i, carry):
        y_copy(i).wait()
        acc_copy(i).wait()
        return carry

    def halo_wait_step(t, carry):
        dhalo_copy(t).wait()
        return carry

    lax.fori_loop(0, blocks, wait_step, 0)
    lax.fori_loop(0, before, halo_wait_step, 0)


def attention(meta, ends, k, kt, x, before):
    blocks, _, rows, dim = x.shape
    group = x.shape[1] // 2
    tiles, _, tile, _ = k.shape
    cuts = rows // tile
    hbm = pl.BlockSpec(memory_space=HBM)
    any_space = pl.BlockSpec(memory_space=pl.ANY)
    most = before * cuts + 1
    return pl.pallas_call(
        functools.partial(attention_kernel, blocks=blocks, before=before, group=group),
        out_shape=(
            jax.ShapeDtypeStruct(x.shape, jnp.bfloat16),
            jax.ShapeDtypeStruct((blocks, 2, rows, dim), jnp.float32),
            jax.ShapeDtypeStruct((before, 2, rows, dim), jnp.bfloat16),
        ),
        in_specs=[SMEM, VMEM, any_space, any_space, any_space],
        out_specs=(any_space, any_space, any_space),
        scratch_shapes=[
            pltpu.VMEM(k.shape, k.dtype),
            pltpu.VMEM(kt.shape, kt.dtype),
            pltpu.VMEM(x.shape, x.dtype),
            pltpu.VMEM((before + blocks, 2, rows, dim), jnp.float32),
            pltpu.VMEM((cuts, most * tile, group * tile), jnp.float32),
            pltpu.VMEM((cuts, most * tile, group * tile), jnp.float32),
            pltpu.VMEM(x.shape, jnp.bfloat16),
            pltpu.VMEM((before, 2, rows, dim), jnp.bfloat16),
            pltpu.SemaphoreType.DMA((blocks,)),
            pltpu.SemaphoreType.DMA((blocks,)),
            pltpu.SemaphoreType.DMA((blocks,)),
            pltpu.SemaphoreType.DMA((blocks,)),
            pltpu.SemaphoreType.DMA((blocks,)),
            pltpu.SemaphoreType.DMA((before,)),
        ],
        compiler_params=pltpu.CompilerParams(vmem_limit_bytes=VMEM_LIMIT),
        cost_estimate=pl.CostEstimate(flops=5 * 10**9, bytes_accessed=12 * 2**20, transcendentals=4 * 10**6),
    )(meta, ends, k, kt, x)


def gather_kernel(k_ref, v_ref, out_ref):
    out_ref[:, 0] = jnp.swapaxes(k_ref[...], 0, 1)
    out_ref[:, 1] = jnp.swapaxes(v_ref[...], 0, 1)


def gather_heads(k, v, part):
    rows, heads, dim = k.shape
    return pl.pallas_call(
        gather_kernel,
        grid=(rows // part,),
        out_shape=jax.ShapeDtypeStruct((heads, 2, rows, dim), k.dtype),
        in_specs=[pl.BlockSpec((part, heads, dim), lambda i: (i, 0, 0))] * 2,
        out_specs=pl.BlockSpec((heads, 2, part, dim), lambda i: (0, 0, i, 0)),
        cost_estimate=pl.CostEstimate(flops=10**6, bytes_accessed=2 * 2**20, transcendentals=0),
    )(k, v)


def scatter_kernel(x_ref, k_ref, v_ref):
    k_ref[...] = jnp.swapaxes(x_ref[:, 0], 0, 1)
    v_ref[...] = jnp.swapaxes(x_ref[:, 1], 0, 1)


def scatter_heads(x, part):
    heads, _, rows, dim = x.shape
    one = jax.ShapeDtypeStruct((rows, heads, dim), x.dtype)
    return pl.pallas_call(
        scatter_kernel,
        grid=(rows // part,),
        out_shape=(one, one),
        in_specs=[pl.BlockSpec((heads, 2, part, dim), lambda i: (0, 0, i, 0))],
        out_specs=(pl.BlockSpec((part, heads, dim), lambda i: (i, 0, 0)),) * 2,
        cost_estimate=pl.CostEstimate(flops=10**6, bytes_accessed=2 * 2**20, transcendentals=0),
    )(x)


def after(array, other):
    return lax.optimization_barrier((array, other))[0]


def body(queries, keys, values, out_grad, doc_lengths):
    rows, heads, dim = queries.shape
    kv_heads = keys.shape[1]
    group = heads // kv_heads
    blocks = kv_heads
    parts = lax.axis_size("ctx") // blocks
    before = WINDOW // rows
    tile = TILE
    turns = [(p % 2) * (blocks // 2) for p in range(parts)]
    groups = [[p * blocks + (r + turns[p]) % blocks for r in range(blocks)] for p in range(parts)]
    onward = [(groups[p][r], groups[p + 1][r]) for p in range(parts - 1) for r in range(blocks)]
    part = lax.axis_index("ctx") // blocks

    docs = doc_lengths.shape[0]
    upto = jnp.arange(docs)[:, None] >= jnp.arange(docs)[None, :]
    ends = jnp.sum(jnp.where(upto, doc_lengths[None, :], 0), axis=1)
    base = part * blocks * rows
    turn = lax.rem(part, 2) * (blocks // 2)
    position = base + jnp.arange(blocks * (rows // tile), dtype=jnp.int32) * tile
    start = jnp.max(jnp.where(ends[None, :] <= position[:, None], ends[None, :], 0), axis=1)
    first = jnp.maximum(jnp.maximum(start, position - (WINDOW - 1)), 0)
    meta = jnp.concatenate((position // tile - first // tile + 1, jnp.stack((base, turn)))).astype(jnp.int32)
    ends = ends[:, None].astype(jnp.int32)

    def exchange(array):
        return lax.all_to_all(array, "ctx", 0, 0, axis_index_groups=groups)

    def by_head(array):
        array = jnp.swapaxes(array, 0, 1)
        return array.reshape(kv_heads, array.shape[0] // kv_heads, array.shape[1], dim)

    def by_token(array):
        array = array.reshape(array.shape[0] * array.shape[1], array.shape[2], dim)
        return jnp.swapaxes(array, 0, 1)

    kv = exchange(gather_heads(keys, values, TILE))
    tail = jnp.stack([kv[(blocks - before + t + turns[0]) % blocks] for t in range(before)]) if turns[0] else kv[blocks - before:]
    halo = lax.ppermute(tail, "ctx", onward)
    packed = jnp.concatenate([by_head(a) for a in (queries, out_grad)], 1)
    x = exchange(after(packed, kv))
    k, kt = prepare(jnp.stack((base, turn)).astype(jnp.int32), kv, halo, tile)
    y, dkv, dhalo = attention(meta, ends, k, kt, x, before)
    dhalo = lax.ppermute(dhalo, "ctx", [(b, a) for a, b in onward])
    y = exchange(y)
    factor = jnp.where(jnp.arange(2) == 0, SCALING, 1.0).astype(jnp.float32)[:, None, None]
    dhalo = jnp.pad(dhalo.astype(jnp.float32), ((blocks - before, 0), (0, 0), (0, 0), (0, 0)))
    dkv = (dkv * factor + dhalo).astype(jnp.bfloat16)
    dkv = exchange(after(dkv, y))
    dk, dv = scatter_heads(dkv, TILE)
    return by_token(y[:, :group]), by_token(y[:, group:]), dk, dv


def solution(mesh):
    spec = P(("dp", "ctx"), "head", None)
    return jax.shard_map(
        body,
        mesh=mesh,
        in_specs=(spec, spec, spec, spec, P("dp")),
        out_specs=(spec, spec, spec, spec),
        check_vma=False,
    )
```

```python
import functools

import jax
import jax.numpy as jnp
from jax import lax
from jax.experimental import pallas as pl
from jax.experimental.pallas import tpu as pltpu
from jax.sharding import PartitionSpec as P

WINDOW = 1024
SCALING = 168.0 ** (-0.5)
LOG2E = 1.4426950408889634
NEG = -1e30
TILE = 128
VMEM_LIMIT = 48 * 1024 * 1024
HBM = pl.ANY
JOINT = (2, 8)

NT = (((1,), (1,)), ((), ()))
NN = (((1,), (0,)), ((), ()))

VMEM = pl.BlockSpec(memory_space=pltpu.VMEM)
SMEM = pl.BlockSpec(memory_space=pltpu.SMEM)


def dot(a, b, dims):
    return lax.dot_general(a, b, dims, preferred_element_type=jnp.float32)


def place(i, turn, blocks):
    return lax.rem(i + turn, blocks)


def prepare_kernel(meta_ref, kv_ref, halo_ref, k_hbm, kt_hbm, k_ref, kt_ref, k_sem, kt_sem, *, blocks, tile):
    before = halo_ref.shape[0]
    cuts = kv_ref.shape[2] // tile
    turn = meta_ref[1]

    def put(source, index, at):
        for n in range(2):
            for c in range(cuts):
                part = source[index, n, c * tile:(c + 1) * tile]
                k_ref[at * cuts + c, n] = part
                kt_ref[at * cuts + c, n] = part.T

    def halo_step(t, carry):
        put(halo_ref, t, t)
        return carry

    def own_step(t, carry):
        put(kv_ref, place(t, turn, blocks), before + t)
        return carry

    lax.fori_loop(0, before, halo_step, 0)
    lax.fori_loop(0, blocks, own_step, 0, unroll=2)
    copies = [pltpu.make_async_copy(k_ref, k_hbm, k_sem), pltpu.make_async_copy(kt_ref, kt_hbm, kt_sem)]
    for copy in copies:
        copy.start()
    for copy in copies:
        copy.wait()


def prepare(meta, kv, halo, tile):
    blocks, _, rows, dim = kv.shape
    tiles = (halo.shape[0] + blocks) * (rows // tile)
    outs = (
        jax.ShapeDtypeStruct((tiles, 2, tile, dim), kv.dtype),
        jax.ShapeDtypeStruct((tiles, 2, dim, tile), kv.dtype),
    )
    hbm = pl.BlockSpec(memory_space=HBM)
    return pl.pallas_call(
        functools.partial(prepare_kernel, blocks=blocks, tile=tile),
        out_shape=outs,
        in_specs=[SMEM, VMEM, VMEM],
        out_specs=(hbm, hbm),
        scratch_shapes=[pltpu.VMEM(o.shape, o.dtype) for o in outs] + [pltpu.SemaphoreType.DMA] * 2,
        compiler_params=pltpu.CompilerParams(vmem_limit_bytes=12 * 1024 * 1024),
        cost_estimate=pl.CostEstimate(flops=10**6, bytes_accessed=6 * 2**20, transcendentals=0),
    )(meta, kv, halo)


def attention_kernel(
    meta_ref, ends_ref, k_hbm, kt_hbm, x_hbm, y_hbm, acc_hbm, dhalo_hbm,
    k_ref, kt_ref, x_ref, acc_ref, s_ref, g_ref, y_ref, dhalo_ref, k_sem, kt_sem, x_sem, y_sem, acc_sem, dhalo_sem, *, blocks, before, group,
):
    rows, dim = x_ref.shape[2:]
    tile = k_ref.shape[2]
    wide = group * tile
    cuts = rows // tile
    halo = before * cuts
    base, turn = meta_ref[blocks * cuts], meta_ref[blocks * cuts + 1]

    def tile_copies(block):
        near = pl.ds(halo + block * cuts, cuts)
        return [pltpu.make_async_copy(h.at[near], r.at[near], sem.at[block]) for h, r, sem in sources]

    sources = ((k_hbm, k_ref, k_sem), (kt_hbm, kt_ref, kt_sem))
    start_copies = [
        pltpu.make_async_copy(h.at[pl.ds(0, halo + cuts)], r.at[pl.ds(0, halo + cuts)], sem.at[0]) for h, r, sem in sources
    ]

    def x_copy(at):
        return pltpu.make_async_copy(x_hbm.at[at], x_ref.at[at], x_sem.at[at])

    x_copy(place(0, turn, blocks)).start()
    for copy in start_copies:
        copy.start()

    def fetch_step(block, carry):
        x_copy(place(block, turn, blocks)).start()
        for copy in tile_copies(block):
            copy.start()
        return carry

    lax.fori_loop(1, blocks, fetch_step, 0)

    def zero_step(t, carry):
        acc_ref[t] = jnp.zeros(acc_ref.shape[1:], jnp.float32)
        return carry

    lax.fori_loop(0, before, zero_step, 0)

    def acc_at(t, m):
        return t // cuts, m, pl.ds(pl.multiple_of(lax.rem(t, cuts) * tile, tile), tile)

    lane = lax.rem(lax.broadcasted_iota(jnp.int32, (1, wide), 1), tile)
    diff = lane - lax.broadcasted_iota(jnp.int32, (2 * tile, wide), 0)

    def y_copy(at):
        return pltpu.make_async_copy(y_ref.at[at], y_hbm.at[at], y_sem.at[at])

    def acc_copy(t):
        return pltpu.make_async_copy(acc_ref.at[before + t], acc_hbm.at[place(t, turn, blocks)], acc_sem.at[t])

    def dhalo_copy(t):
        return pltpu.make_async_copy(dhalo_ref.at[t], dhalo_hbm.at[t], dhalo_sem.at[t])

    def scores(slot, i, at, piece, count):
        first = halo + i - (count - 1)
        span = pl.ds(piece * tile, tile)
        q = x_ref[at, 0:group, span].reshape(wide, dim)
        do = x_ref[at, group:2 * group, span].reshape(wide, dim)
        pos = base + i * tile + lane
        ends = ends_ref[...]
        start = jnp.max(jnp.where(ends <= pos, ends, 0), axis=0, keepdims=True)
        reach = pos - jnp.maximum(start, pos - (WINDOW - 1))
        chunks = [(0, 1)] * (count % 2) + [(a, 2) for a in range(count % 2, count, 2)]
        top = None
        for a, n in chunks:
            raw = dot(k_ref[pl.ds(first + a, n), 0].reshape(n * tile, dim), q, NT)
            offset = (count - 1 - a) * tile
            keep = diff[:n * tile] <= reach - offset
            if a + n == count:
                keep = keep & (diff[:n * tile] >= -offset)
            raw = jnp.where(keep, raw, NEG)
            s_ref[slot, a * tile:(a + n) * tile] = raw
            here = jnp.max(raw, axis=0, keepdims=True)
            top = here if top is None else jnp.maximum(top, here)
            g_ref[slot, a * tile:(a + n) * tile] = dot(
                k_ref[pl.ds(first + a, n), 1].reshape(n * tile, dim), do, NT
            )
        return first, q, do, chunks, top

    def weigh(slot, state):
        first, q, do, chunks, top = state
        total = mixed = 0.0
        for a, n in chunks:
            p = jnp.exp2((s_ref[slot, a * tile:(a + n) * tile] - top) * (SCALING * LOG2E))
            s_ref[slot, a * tile:(a + n) * tile] = p
            total += jnp.sum(p, axis=0, keepdims=True)
            mixed += jnp.sum(p * g_ref[slot, a * tile:(a + n) * tile], axis=0, keepdims=True)
        inverse = 1.0 / total
        return first, q, do, chunks, inverse, mixed * inverse

    def gradients(slot, at, piece, count, state):
        first, q, do, chunks, inverse, row_total = state
        span = pl.ds(piece * tile, tile)
        out = dq = 0.0
        for a, n in chunks:
            w = s_ref[slot, a * tile:(a + n) * tile] * inverse
            wb = w.astype(jnp.bfloat16)
            ds = (w * (g_ref[slot, a * tile:(a + n) * tile] - row_total)).astype(jnp.bfloat16)
            kt, vt = (
                jnp.concatenate([kt_ref[first + a + c, m] for c in range(n)], axis=1) for m in range(2)
            )
            out += dot(vt, wb, NN)
            dq += dot(kt, ds, NN)
            for m, part in enumerate((dot(ds, q, NN), dot(wb, do, NN))):
                for c in range(n):
                    here = acc_at(first + a + c, m)
                    if a + c == count - 1:
                        acc_ref[here] = part[c * tile:]
                    else:
                        acc_ref[here] += part[c * tile:(c + 1) * tile]
        y_ref[at, 0:group, span] = out.T.astype(jnp.bfloat16).reshape(group, tile, dim)
        y_ref[at, group:2 * group, span] = (SCALING * dq).T.astype(jnp.bfloat16).reshape(group, tile, dim)

    def query_tiles(block, at, pieces, count):
        states = [scores(slot, block * cuts + c, at, c, count) for slot, c in enumerate(pieces)]
        states = [weigh(slot, state) for slot, state in enumerate(states)]
        for slot, c in enumerate(pieces):
            gradients(slot, at, c, count, states[slot])

    def block_step(block, carry):
        at = place(block, turn, blocks)
        counts = [meta_ref[block * cuts + c] for c in range(cuts)]
        most = functools.reduce(jnp.maximum, counts)
        x_copy(at).wait()

        @pl.when(block == 0)
        def _():
            for copy in start_copies:
                copy.wait()

        @pl.when(block > 0)
        def _():
            for copy in tile_copies(block):
                copy.wait()

        for n in range(JOINT[0], JOINT[1]):
            here = (most == n) if n > JOINT[0] else (most <= n)
            pl.when(here)(functools.partial(query_tiles, block, at, list(range(cuts)), n))
        for c in range(cuts):
            for n in range(1, halo + 2):
                here = (counts[c] == n) & (most >= JOINT[1])
                pl.when(here)(functools.partial(query_tiles, block, at, [c], n))
        y_copy(at).start()

        @pl.when(block < before)
        def _():
            dhalo_ref[block, 0] = (SCALING * acc_ref[block, 0]).astype(jnp.bfloat16)
            dhalo_ref[block, 1] = acc_ref[block, 1].astype(jnp.bfloat16)
            dhalo_copy(block).start()

        @pl.when(block >= before)
        def _():
            acc_copy(block - before).start()

        return carry

    lax.fori_loop(0, blocks, block_step, 0)
    for t in range(blocks - before, blocks):
        acc_copy(t).start()

    def wait_step(i, carry):
        y_copy(i).wait()
        acc_copy(i).wait()
        return carry

    def halo_wait_step(t, carry):
        dhalo_copy(t).wait()
        return carry

    lax.fori_loop(0, blocks, wait_step, 0)
    lax.fori_loop(0, before, halo_wait_step, 0)


def attention(meta, ends, k, kt, x, before):
    blocks, _, rows, dim = x.shape
    group = x.shape[1] // 2
    tiles, _, tile, _ = k.shape
    cuts = rows // tile
    hbm = pl.BlockSpec(memory_space=HBM)
    any_space = pl.BlockSpec(memory_space=pl.ANY)
    most = before * cuts + 1
    return pl.pallas_call(
        functools.partial(attention_kernel, blocks=blocks, before=before, group=group),
        out_shape=(
            jax.ShapeDtypeStruct(x.shape, jnp.bfloat16),
            jax.ShapeDtypeStruct((blocks, 2, rows, dim), jnp.float32),
            jax.ShapeDtypeStruct((before, 2, rows, dim), jnp.bfloat16),
        ),
        in_specs=[SMEM, VMEM, any_space, any_space, any_space],
        out_specs=(any_space, any_space, any_space),
        scratch_shapes=[
            pltpu.VMEM(k.shape, k.dtype),
            pltpu.VMEM(kt.shape, kt.dtype),
            pltpu.VMEM(x.shape, x.dtype),
            pltpu.VMEM((before + blocks, 2, rows, dim), jnp.float32),
            pltpu.VMEM((cuts, most * tile, group * tile), jnp.float32),
            pltpu.VMEM((cuts, most * tile, group * tile), jnp.float32),
            pltpu.VMEM(x.shape, jnp.bfloat16),
            pltpu.VMEM((before, 2, rows, dim), jnp.bfloat16),
            pltpu.SemaphoreType.DMA((blocks,)),
            pltpu.SemaphoreType.DMA((blocks,)),
            pltpu.SemaphoreType.DMA((blocks,)),
            pltpu.SemaphoreType.DMA((blocks,)),
            pltpu.SemaphoreType.DMA((blocks,)),
            pltpu.SemaphoreType.DMA((before,)),
        ],
        compiler_params=pltpu.CompilerParams(vmem_limit_bytes=VMEM_LIMIT),
        cost_estimate=pl.CostEstimate(flops=5 * 10**9, bytes_accessed=12 * 2**20, transcendentals=4 * 10**6),
    )(meta, ends, k, kt, x)


def gather_kernel(k_ref, v_ref, out_ref):
    out_ref[:, 0] = jnp.swapaxes(k_ref[...], 0, 1)
    out_ref[:, 1] = jnp.swapaxes(v_ref[...], 0, 1)


def gather_heads(k, v, part):
    rows, heads, dim = k.shape
    return pl.pallas_call(
        gather_kernel,
        grid=(rows // part,),
        out_shape=jax.ShapeDtypeStruct((heads, 2, rows, dim), k.dtype),
        in_specs=[pl.BlockSpec((part, heads, dim), lambda i: (i, 0, 0))] * 2,
        out_specs=pl.BlockSpec((heads, 2, part, dim), lambda i: (0, 0, i, 0)),
        cost_estimate=pl.CostEstimate(flops=10**6, bytes_accessed=2 * 2**20, transcendentals=0),
    )(k, v)


def scatter_kernel(x_ref, k_ref, v_ref):
    k_ref[...] = jnp.swapaxes(x_ref[:, 0], 0, 1)
    v_ref[...] = jnp.swapaxes(x_ref[:, 1], 0, 1)


def scatter_heads(x, part):
    heads, _, rows, dim = x.shape
    one = jax.ShapeDtypeStruct((rows, heads, dim), x.dtype)
    return pl.pallas_call(
        scatter_kernel,
        grid=(rows // part,),
        out_shape=(one, one),
        in_specs=[pl.BlockSpec((heads, 2, part, dim), lambda i: (0, 0, i, 0))],
        out_specs=(pl.BlockSpec((part, heads, dim), lambda i: (i, 0, 0)),) * 2,
        cost_estimate=pl.CostEstimate(flops=10**6, bytes_accessed=2 * 2**20, transcendentals=0),
    )(x)


def after(array, other):
    return lax.optimization_barrier((array, other))[0]


def body(queries, keys, values, out_grad, doc_lengths):
    rows, heads, dim = queries.shape
    kv_heads = keys.shape[1]
    group = heads // kv_heads
    blocks = kv_heads
    parts = lax.axis_size("ctx") // blocks
    before = WINDOW // rows
    tile = TILE
    turns = [(p % 2) * (blocks // 2) for p in range(parts)]
    groups = [[p * blocks + (r + turns[p]) % blocks for r in range(blocks)] for p in range(parts)]
    onward = [(groups[p][r], groups[p + 1][r]) for p in range(parts - 1) for r in range(blocks)]
    part = lax.axis_index("ctx") // blocks

    docs = doc_lengths.shape[0]
    upto = jnp.arange(docs)[:, None] >= jnp.arange(docs)[None, :]
    ends = jnp.sum(jnp.where(upto, doc_lengths[None, :], 0), axis=1)
    base = part * blocks * rows
    turn = lax.rem(part, 2) * (blocks // 2)
    position = base + jnp.arange(blocks * (rows // tile), dtype=jnp.int32) * tile
    start = jnp.max(jnp.where(ends[None, :] <= position[:, None], ends[None, :], 0), axis=1)
    first = jnp.maximum(jnp.maximum(start, position - (WINDOW - 1)), 0)
    meta = jnp.concatenate((position // tile - first // tile + 1, jnp.stack((base, turn)))).astype(jnp.int32)
    ends = ends[:, None].astype(jnp.int32)

    def exchange(array):
        return lax.all_to_all(array, "ctx", 0, 0, axis_index_groups=groups)

    def by_head(array):
        array = jnp.swapaxes(array, 0, 1)
        return array.reshape(kv_heads, array.shape[0] // kv_heads, array.shape[1], dim)

    def by_token(array):
        array = array.reshape(array.shape[0] * array.shape[1], array.shape[2], dim)
        return jnp.swapaxes(array, 0, 1)

    kv = exchange(gather_heads(keys, values, TILE))
    tail = jnp.stack([kv[(blocks - before + t + turns[0]) % blocks] for t in range(before)]) if turns[0] else kv[blocks - before:]
    halo = lax.ppermute(tail, "ctx", onward)
    packed = jnp.concatenate([by_head(a) for a in (queries, out_grad)], 1)
    x = exchange(after(packed, kv))
    k, kt = prepare(jnp.stack((base, turn)).astype(jnp.int32), kv, halo, tile)
    y, dkv, dhalo = attention(meta, ends, k, kt, x, before)
    dhalo = lax.ppermute(dhalo, "ctx", [(b, a) for a, b in onward])
    y = exchange(y)
    factor = jnp.where(jnp.arange(2) == 0, SCALING, 1.0).astype(jnp.float32)[:, None, None]
    dhalo = jnp.pad(dhalo.astype(jnp.float32), ((blocks - before, 0), (0, 0), (0, 0), (0, 0)))
    dkv = (dkv * factor + dhalo).astype(jnp.bfloat16)
    dkv = exchange(after(dkv, y))
    dk, dv = scatter_heads(dkv, TILE)
    return by_token(y[:, :group]), by_token(y[:, group:]), dk, dv


def solution(mesh):
    spec = P(("dp", "ctx"), "head", None)
    return jax.shard_map(
        body,
        mesh=mesh,
        in_specs=(spec, spec, spec, spec, P("dp")),
        out_specs=(spec, spec, spec, spec),
        check_vma=False,
    )
```
